32 devices in a mesh: ctx: 8 (over z, y), head: 4 (over x, core).
Axes of the slice: x: 2, y: 2, z: 4, core: 2. Of those that a mesh axis runs over, the one named last changes fastest.
Arguments:
- queries: bfloat16 [8192, 64, 128], P('ctx', 'head'), may hold values from -8 to 8
- key_rows: bfloat16 [8192, 64, 128], P('ctx', 'head'), may hold values from -4 to 4
- value_rows: bfloat16 [8192, 64, 128], P('ctx', 'head'), may hold values from -12 to 12
- grad_normed: bfloat16 [8192, 64, 128], P('ctx', 'head'), may hold values from -6 to 6
- norm_gain: float32 [64, 128], P('head'), may hold values from 0.1 to 1.9
- document_starts: int32 [6], replicated, may hold values from 0 to 8064, as said below
Outputs:
- normed: bfloat16 [8192, 64, 128], P('ctx', 'head')
- grad_queries: bfloat16 [8192, 64, 128], P('ctx', 'head')
- grad_keys: bfloat16 [8192, 64, 128], P('ctx', 'head')
- grad_values: bfloat16 [8192, 64, 128], P('ctx', 'head')
- grad_gain: float32 [64, 128], P('head')
The draws below stay inside these ranges and needn't reach their ends.
Inputs may be any that keep to these rules, and one draw needn't show every extreme that they name: `document_starts`: strictly increasing multiples of 128; the first is 0 and the last is 8064.
All inputs are finite; a program needn't handle non-finite values.
Results may differ from the reference program's by a relative error of at most 0.0057.
Values sent between devices are 32-bit elements; how exact they have to be, the bound alone decides.
No kernel may reach another device: no remote copies, remote signals or barrier semaphores. Data moves between devices by JAX's collectives and lax.ppermute only.
A program may use at most 192 MiB of HBM per device.

```python
import math
import jax
import jax.numpy as jnp
from jax import lax

HEADS = 64
HEAD_DIM = 128
TILE = 512
ALIGN = 128
DOCS = 6
TOKENS = 8192


def rough_entries(entry_key, shape):
    return jax.random.normal(entry_key, shape, jnp.float32)


def draw_queries(key, part):
    entry_key, row_key = jax.random.split(jax.random.fold_in(key, 11), 2)
    entries = rough_entries(entry_key, (TOKENS, HEADS, HEAD_DIM))
    row_scale = jnp.exp(jax.random.uniform(row_key, (TOKENS, 1, 1), jnp.float32, 0.0, math.log(10.0)))
    return jnp.clip(entries * row_scale * HEAD_DIM ** (-0.25), -8.0, 8.0).astype(jnp.bfloat16)


def draw_value_rows(key, part):
    entry_key, row_key, jitter_key = jax.random.split(jax.random.fold_in(key, 23), 3)
    entries = rough_entries(entry_key, (TOKENS, HEADS, HEAD_DIM))
    spread = math.log(3.0)
    head_steps = jnp.arange(HEADS, dtype=jnp.float32) / (HEADS - 1)
    jitter = jax.random.uniform(jitter_key, (HEADS,), jnp.float32, -0.3, 0.3)
    head_scale = jnp.exp(spread * head_steps + jitter)[None, :, None]
    row_scale = jnp.exp(jax.random.uniform(row_key, (TOKENS, 1, 1), jnp.float32, 0.0, math.log(3.0)))
    return jnp.clip(entries * head_scale * row_scale, -12.0, 12.0).astype(jnp.bfloat16)


def draw_grad_normed(key, part):
    entry_key, row_key = jax.random.split(jax.random.fold_in(key, 37), 2)
    entries = rough_entries(entry_key, (TOKENS, HEADS, HEAD_DIM))
    row_scale = jnp.exp(jax.random.uniform(row_key, (TOKENS, 1, 1), jnp.float32, 0.0, math.log(3.0)))
    rising = jnp.exp(math.log(3.0) * jnp.arange(TOKENS, dtype=jnp.float32) / (TOKENS - 1))[:, None, None]
    return jnp.clip(0.3 * entries * row_scale * rising, -6.0, 6.0).astype(jnp.bfloat16)


def draw_document_starts(key, part):
    block_count = TOKENS // ALIGN
    shuffled = jax.random.permutation(jax.random.fold_in(key, 41), block_count - 2) + 1
    inner = jnp.sort(shuffled[:DOCS - 2])
    first_block = jnp.zeros((1,), jnp.int32)
    final_block = jnp.full((1,), block_count - 1, jnp.int32)
    return (jnp.concatenate([first_block, inner.astype(jnp.int32), final_block]) * ALIGN).astype(jnp.int32)


def shard_levels(own_key, dims, shards, smallest, largest):
    factor_of = 1.0
    for axis_at, blocks in shards:
        heights = jax.random.uniform(jax.random.fold_in(jax.random.fold_in(own_key, 6), axis_at), (blocks,), jnp.float32, smallest / len(shards), largest / len(shards))
        factor_of = factor_of * jnp.repeat(jnp.exp(heights), dims[axis_at] // blocks).reshape((-1,) + (1,) * (len(dims) - 1 - axis_at))
    return factor_of


def gaussian(stream_key, extent, scale, bound, shards=(), kind=jnp.bfloat16):
    values = scale * jax.random.normal(stream_key, extent, jnp.float32)
    if shards:
        values = values * shard_levels(stream_key, extent, shards, -0.22, 0.18)
    return jnp.clip(values, -bound, bound).astype(kind)


def setup_inputs(seed: int = 0) -> dict:
    streams_of = jax.random.split(jax.random.key(seed), 7)
    queries = draw_queries(jax.random.fold_in(streams_of[6], 71), 0)
    key_rows = gaussian(streams_of[1], (TOKENS, HEADS, HEAD_DIM), (HEAD_DIM ** -0.25), 4.0, ((0, 8), (1, 4)))
    value_rows = draw_value_rows(jax.random.fold_in(streams_of[6], 71), 0)
    grad_normed = draw_grad_normed(jax.random.fold_in(streams_of[6], 71), 0)
    norm_gain = jnp.clip(1.0 + 0.18 * jax.random.normal(streams_of[4], (HEADS, HEAD_DIM), jnp.float32), 0.1, 1.9)
    document_starts = draw_document_starts(jax.random.fold_in(streams_of[6], 71), 0)
    return {"queries": queries, "key_rows": key_rows, "value_rows": value_rows, "grad_normed": grad_normed, "norm_gain": norm_gain, "document_starts": document_starts}


EPSILON = 1e-06

def token_documents(starts, positions):
    return lax.optimization_barrier(jnp.sum((starts[None, :] <= positions[:, None]).astype(jnp.int32), axis=1)).astype(jnp.int32) - 1

def rounded(array):
    return lax.optimization_barrier(array.astype(jnp.bfloat16)).astype(jnp.float32)

def reference(queries, key_rows, value_rows, grad_normed, norm_gain, document_starts):
    tile_count = TOKENS // TILE
    feature_count = HEADS * HEAD_DIM
    positions = jnp.arange(TOKENS, dtype=jnp.int32)
    documents = token_documents(document_starts, positions).reshape(tile_count, TILE)
    prior_docs = token_documents(document_starts, jnp.arange(tile_count, dtype=jnp.int32) * TILE - 1)
    last_docs = documents[:, -1]
    causal = jnp.arange(TILE)[:, None] >= jnp.arange(TILE)[None, :]

    def shaped(array):
        return array.reshape(tile_count, TILE, HEADS, HEAD_DIM)

    def tile_masks(tile_docs, prior_doc, last_doc):
        entering = (tile_docs == prior_doc).astype(jnp.float32)
        leaving = (tile_docs == last_doc).astype(jnp.float32)
        within = (causal & (tile_docs[:, None] == tile_docs[None, :])).astype(jnp.float32)
        keep_flag = (last_doc == prior_doc).astype(jnp.float32)
        return (entering, leaving, within, keep_flag)

    def forward_step(carried_in, inputs):
        carried, gain_sum = carried_in
        query_tile, key_tile, value_tile, upstream_tile, tile_docs, prior_doc, last_doc = inputs
        entering, leaving, within, keep_flag = tile_masks(tile_docs, prior_doc, last_doc)
        query_f = query_tile.astype(jnp.float32)
        key_f = key_tile.astype(jnp.float32)
        value_f = value_tile.astype(jnp.float32)
        attention = rounded(jnp.einsum('thd,shd->hts', query_f, key_f) * within[None])
        state_bf = rounded(carried)
        intra_out = jnp.einsum('hts,shd->thd', attention, value_f)
        inter_out = jnp.einsum('thd,hde->the', query_f, state_bf)
        attended = intra_out + entering[:, None, None] * inter_out
        squares = lax.optimization_barrier(jnp.sum(attended * attended, axis=(1, 2)))
        inverse = 1.0 / jnp.sqrt(squares / feature_count + EPSILON)
        scaled = attended * inverse[:, None, None]
        normed = (scaled * norm_gain).astype(jnp.bfloat16)
        upstream = upstream_tile.astype(jnp.float32)
        weighted = upstream * norm_gain
        cross_sum = lax.optimization_barrier(jnp.sum(weighted * attended, axis=(1, 2)))
        grad_att = rounded(inverse[:, None, None] * weighted - attended * (inverse ** 3 * cross_sum / feature_count)[:, None, None])
        grad_scores = rounded(jnp.einsum('the,she->hts', grad_att, value_f) * within[None])
        query_intra = jnp.einsum('hts,shd->thd', grad_scores, key_f)
        query_inter = jnp.einsum('the,hde->thd', grad_att, state_bf)
        grad_query = (query_intra + entering[:, None, None] * query_inter).astype(jnp.bfloat16)
        tile_state = jnp.einsum('thd,the->hde', key_f * leaving[:, None, None], value_f)
        next_state = tile_state + keep_flag * carried
        gain_sum = gain_sum + lax.optimization_barrier(jnp.sum(upstream * scaled, axis=0))
        return ((next_state, gain_sum), (normed, grad_att.astype(jnp.bfloat16), grad_query))
    inputs = (shaped(queries), shaped(key_rows), shaped(value_rows), shaped(grad_normed), documents, prior_docs, last_docs)
    start_state = jnp.zeros((HEADS, HEAD_DIM, HEAD_DIM), jnp.float32)
    start_gain = jnp.zeros((HEADS, HEAD_DIM), jnp.float32)
    (final_state, gain_sum), (normed, grad_att, grad_queries) = lax.scan(forward_step, (start_state, start_gain), inputs)

    def backward_step(exit_state, inputs_back):
        query_tile, key_tile, value_tile, grad_tile, tile_docs, prior_doc, last_doc = inputs_back
        entering, leaving, within, keep_flag = tile_masks(tile_docs, prior_doc, last_doc)
        query_f = query_tile.astype(jnp.float32)
        key_f = key_tile.astype(jnp.float32)
        value_f = value_tile.astype(jnp.float32)
        grad_f = grad_tile.astype(jnp.float32)
        attention = rounded(jnp.einsum('thd,shd->hts', query_f, key_f) * within[None])
        grad_scores = rounded(jnp.einsum('the,she->hts', grad_f, value_f) * within[None])
        exit_bf = rounded(exit_state)
        key_intra = jnp.einsum('hts,thd->shd', grad_scores, query_f)
        key_inter = jnp.einsum('she,hde->shd', value_f, exit_bf)
        value_intra = jnp.einsum('hts,the->she', attention, grad_f)
        value_inter = jnp.einsum('shd,hde->she', key_f, exit_bf)
        grad_key = (key_intra + leaving[:, None, None] * key_inter).astype(jnp.bfloat16)
        grad_value = (value_intra + leaving[:, None, None] * value_inter).astype(jnp.bfloat16)
        tile_grad = jnp.einsum('thd,the->hde', query_f * entering[:, None, None], grad_f)
        earlier_state = tile_grad + keep_flag * exit_state
        return (earlier_state, (grad_key, grad_value))
    inputs_back = (shaped(queries), shaped(key_rows), shaped(value_rows), grad_att, documents, prior_docs, last_docs)
    first_grad, (grad_keys, grad_values) = lax.scan(backward_step, start_state, inputs_back, reverse=True)
    whole = (TOKENS, HEADS, HEAD_DIM)
    grad_gain = gain_sum / math.sqrt(TOKENS)
    return (normed.reshape(whole), grad_queries.reshape(whole), grad_keys.reshape(whole), grad_values.reshape(whole), grad_gain)
```

```python
import functools
import math

import jax
import jax.numpy as jnp
from jax import lax
from jax.experimental import pallas as pl
from jax.experimental.pallas import tpu as pltpu
from jax.sharding import PartitionSpec as P

CHUNK = 256
LANES = 128
EPSILON = 1e-06
FAR = 2**30
VMEM_LIMIT = 56 * 1024 * 1024

F32 = jnp.float32
BF16 = jnp.bfloat16


def dot_nn(a, b):
    return lax.dot_general(a, b, (((1,), (0,)), ((), ())), preferred_element_type=F32)


def dot_nt(a, b):
    return lax.dot_general(a, b, (((1,), (1,)), ((), ())), preferred_element_type=F32)


def dot_tn(a, b):
    return lax.dot_general(a, b, (((0,), (0,)), ((), ())), preferred_element_type=F32)


def first_start_from(starts, row):
    best = jnp.int32(FAR)
    for i in range(starts.shape[0]):
        best = jnp.minimum(best, jnp.where(starts[i] >= row, starts[i], FAR))
    return best


def last_start_to(starts, row):
    best = jnp.int32(0)
    for i in range(starts.shape[0]):
        best = jnp.maximum(best, jnp.where(starts[i] <= row, starts[i], 0))
    return best


def token_rows(first, shape, axis):
    return first + lax.broadcasted_iota(jnp.int32, shape, axis)


def within_mask(starts, first, axis):
    shape = (CHUNK, CHUNK)
    t = token_rows(first, shape, axis)
    s = token_rows(first, shape, 1 - axis)
    begin = jnp.zeros(shape, jnp.int32)
    for i in range(starts.shape[0]):
        begin = jnp.maximum(begin, jnp.where(starts[i] <= t, starts[i], 0))
    return jnp.where((s <= t) & (s >= begin), 1.0, 0.0).astype(BF16)


def before_mask(first, bound, dtype):
    return jnp.where(token_rows(first, (CHUNK, LANES), 0) < bound, 1.0, 0.0).astype(dtype)


def from_mask(first, bound, dtype):
    return jnp.where(token_rows(first, (CHUNK, LANES), 0) >= bound, 1.0, 0.0).astype(dtype)


def own_head(base, j, heads):
    return lax.rem(j + base[1] * (heads // 2), heads)


def spread(scratch, block):
    scratch[...] = block[...].astype(F32).reshape(scratch.shape)


def gather_rows(scratch, head, heads):
    return scratch[pl.ds(head, CHUNK, heads), :]


def state_kernel(starts, base, k_ref, v_ref, o0, o1, o2, o3, k_rows, v_rows, total):
    heads = k_ref.shape[1]
    step, steps = pl.program_id(0), pl.num_programs(0)
    first = base[0] + step * CHUNK
    bound = last_start_to(starts, base[0] + steps * CHUNK - 1)

    @pl.when(step == 0)
    def _():
        total[...] = jnp.zeros_like(total)

    @pl.when(bound < first + CHUNK)
    def _():
        spread(k_rows, k_ref)
        spread(v_rows, v_ref)
        leave = from_mask(first, bound, F32)

        def body(j, carry):
            head = own_head(base, j, heads)
            key = (gather_rows(k_rows, head, heads) * leave).astype(BF16)
            value = gather_rows(v_rows, head, heads).astype(BF16)
            total[j] += dot_tn(key, value)
            return carry

        lax.fori_loop(0, heads, body, 0, unroll=4)

    @pl.when(step == steps - 1)
    def _():
        part = heads // 4
        for i, out in enumerate((o0, o1, o2, o3)):
            out[...] = total[i * part : (i + 1) * part]


def turn_kernel(base, *refs):
    count = len(refs) // 3
    ins, outs, rows = refs[:count], refs[count : 2 * count], refs[2 * count :]
    heads = ins[0].shape[1]
    for source, out, scratch in zip(ins, outs, rows):
        spread(scratch, source)

        def body(j, carry, out=out, scratch=scratch):
            out[j] = gather_rows(scratch, own_head(base, j, heads), heads).astype(BF16)
            return carry

        lax.fori_loop(0, heads, body, 0, unroll=4)


def local_kernel(starts, base, q_ref, k_ref, v_ref, att_ref, entry_ref, state, mask, enter, leave):
    heads = q_ref.shape[0]
    step = pl.program_id(0)
    first = base[0] + step * CHUNK
    enter_end = first_start_from(starts, first)
    leave_start = last_start_to(starts, first + CHUNK - 1)
    keep = jnp.where(enter_end >= first + CHUNK, 1.0, 0.0).astype(F32)

    @pl.when(step == 0)
    def _():
        state[...] = jnp.zeros_like(state)

    mask[...] = within_mask(starts, first, 0)
    enter[...] = before_mask(first, enter_end, BF16)
    leave[...] = from_mask(first, leave_start, BF16)

    def body(j, carry):
        query, key, value = q_ref[j], k_ref[j], v_ref[j]
        entry = state[j].astype(BF16)
        entry_ref[0, j] = entry
        scores = dot_nt(query, key).astype(BF16) * mask[...]
        att_ref[j] = (dot_nn(scores, value) + dot_nn(query * enter[...], entry)).astype(att_ref.dtype)
        state[j] = keep * state[j] + dot_tn(key * leave[...], value)
        return carry

    lax.fori_loop(0, heads, body, 0, unroll=2)


def load_states(parts, held):
    part = parts[0].shape[0]
    for i, ref in enumerate(parts):
        held[i * part : (i + 1) * part] = ref[...].astype(held.dtype)


def eye():
    shape = (LANES, LANES)
    return lax.broadcasted_iota(jnp.int32, shape, 0) == lax.broadcasted_iota(jnp.int32, shape, 1)


def column_of(row):
    return jnp.sum(jnp.where(eye(), row, 0.0), axis=1, keepdims=True)


def row_of(column):
    return jnp.sum(jnp.where(eye(), column, 0.0), axis=0, keepdims=True)


def sums_kernel(starts, base, q_ref, att_ref, g_ref, gain, r0, r1, r2, r3, sums, held, squares, cross, enter):
    heads = q_ref.shape[0]
    step, steps = pl.program_id(0), pl.num_programs(0)
    first = base[0] + step * CHUNK

    @pl.when(step == 0)
    def _():
        load_states((r0, r1, r2, r3), held)

    enter[...] = before_mask(first, first_start_from(starts, base[0]), BF16)
    squares[...] = jnp.zeros_like(squares)
    cross[...] = jnp.zeros_like(cross)

    def body(j, carry):
        head = own_head(base, j, heads)
        att = att_ref[j].astype(F32) + dot_nn(q_ref[j] * enter[...], held[j])
        weighted = g_ref[j].astype(F32) * gain[pl.ds(head, 1), :]
        squares[...] += att * att
        cross[...] += weighted * att
        return carry

    lax.fori_loop(0, heads, body, 0, unroll=2)
    blocks = CHUNK // LANES
    for i in range(blocks):
        rows = slice(i * LANES, (i + 1) * LANES)
        place = step * blocks + i
        sums[pl.ds(place, 1), :] = row_of(jnp.sum(squares[rows, :], axis=1, keepdims=True))
        sums[pl.ds(steps * blocks + place, 1), :] = row_of(
            jnp.sum(cross[rows, :], axis=1, keepdims=True)
        )


def norm_columns(sums, step, steps, features, inverse, factor):
    blocks = CHUNK // LANES
    for i in range(blocks):
        rows = slice(i * LANES, (i + 1) * LANES)
        place = step * blocks + i
        square = sums[pl.ds(place, 1), :]
        cross = sums[pl.ds(steps * blocks + place, 1), :]
        inv = 1.0 / jnp.sqrt(square / features + EPSILON)
        fac = inv * inv * inv * cross / features
        inverse[rows, :] = jnp.broadcast_to(column_of(inv), (LANES, LANES))
        factor[rows, :] = jnp.broadcast_to(column_of(fac), (LANES, LANES))


def exit_kernel(
    features, starts, base, q_ref, att_ref, g_ref, gain, sums, r0, r1, r2, r3,
    o0, o1, o2, o3, held, inverse, factor, enter, total,
):
    heads = q_ref.shape[0]
    step, steps = pl.program_id(0), pl.num_programs(0)
    first = base[0] + step * CHUNK
    bound = first_start_from(starts, base[0])

    @pl.when(step == 0)
    def _():
        load_states((r0, r1, r2, r3), held)
        total[...] = jnp.zeros_like(total)

    @pl.when(bound > first)
    def _():
        norm_columns(sums, step, steps, features, inverse, factor)
        enter[...] = before_mask(first, bound, BF16)

        def body(j, carry):
            head = own_head(base, j, heads)
            query = q_ref[j] * enter[...]
            att = att_ref[j].astype(F32) + dot_nn(query, held[j])
            weighted = g_ref[j].astype(F32) * gain[pl.ds(head, 1), :]
            grad = (inverse[...] * weighted - att * factor[...]).astype(BF16)
            total[j] += dot_tn(query, grad)
            return carry

        lax.fori_loop(0, heads, body, 0, unroll=2)

    @pl.when(step == steps - 1)
    def _():
        part = heads // 4
        for i, out in enumerate((o0, o1, o2, o3)):
            out[...] = total[i * part : (i + 1) * part]


def query_kernel(
    features, starts, base, q_ref, k_ref, v_ref, att_ref, g_ref, entry_ref, gain, sums, r0, r1, r2, r3,
    normed, grad_q, grad_att, gain_sum,
    held, inverse, factor, enter, enter_all, mask, norm_rows, grad_rows, gain_total,
):
    heads = q_ref.shape[0]
    step, steps = pl.program_id(0), pl.num_programs(0)
    first = base[0] + step * CHUNK
    bound = first_start_from(starts, base[0])
    reach = jnp.where(bound >= first, 1.0, 0.0).astype(F32)

    @pl.when(step == 0)
    def _():
        load_states((r0, r1, r2, r3), held)
        gain_total[...] = jnp.zeros_like(gain_total)

    norm_columns(sums, step, steps, features, inverse, factor)
    enter_all[...] = before_mask(first, bound, BF16)
    enter[...] = before_mask(first, first_start_from(starts, first), F32)
    mask[...] = within_mask(starts, first, 0)

    def body(j, carry):
        head = own_head(base, j, heads)
        scale = gain[pl.ds(head, 1), :]
        state = held[j]
        att = att_ref[j].astype(F32) + dot_nn(q_ref[j] * enter_all[...], state.astype(BF16))
        upstream = g_ref[j].astype(F32)
        scaled = att * inverse[...]
        norm_rows[pl.ds(head, CHUNK, heads), :] = scaled * scale
        gain_total[pl.ds(head, 1), :] += jnp.sum(upstream * scaled, axis=0, keepdims=True)
        grad = (inverse[...] * (upstream * scale) - att * factor[...]).astype(BF16)
        grad_att[j] = grad
        entry = (entry_ref[0, j].astype(F32) + reach * state).astype(BF16)
        scores = dot_nt(grad, v_ref[j]).astype(BF16) * mask[...]
        grad_rows[pl.ds(head, CHUNK, heads), :] = dot_nn(scores, k_ref[j]) + enter[...] * dot_nt(grad, entry)
        return carry

    lax.fori_loop(0, heads, body, 0, unroll=2)
    normed[...] = norm_rows[...].reshape(normed.shape).astype(BF16)
    grad_q[...] = grad_rows[...].reshape(grad_q.shape).astype(BF16)

    @pl.when(step == steps - 1)
    def _():
        gain_sum[...] = gain_total[...]


def key_kernel(
    starts, base, q_ref, k_ref, v_ref, grad_ref, grad_k, grad_v, state, mask, enter, leave
):
    heads = q_ref.shape[0]
    step, steps = pl.program_id(0), pl.num_programs(0)
    first = base[0] + (steps - 1 - step) * CHUNK
    enter_end = first_start_from(starts, first)
    leave_start = last_start_to(starts, first + CHUNK - 1)
    keep = jnp.where(enter_end >= first + CHUNK, 1.0, 0.0).astype(F32)

    @pl.when(step == 0)
    def _():
        state[...] = jnp.zeros_like(state)

    mask[...] = within_mask(starts, first, 1)
    enter[...] = before_mask(first, enter_end, BF16)
    leave[...] = from_mask(first, leave_start, BF16)

    def body(j, carry):
        query, key, value, grad = q_ref[j], k_ref[j], v_ref[j], grad_ref[j]
        exits = state[j].astype(BF16)
        scores = dot_nt(key, query).astype(BF16) * mask[...]
        grad_v[j] = (dot_nn(scores, grad) + dot_nn(key * leave[...], exits)).astype(grad_v.dtype)
        scores = dot_nt(value, grad).astype(BF16) * mask[...]
        grad_k[j] = (dot_nn(scores, query) + dot_nt(value * leave[...], exits)).astype(grad_k.dtype)
        state[j] = keep * state[j] + dot_tn(query * enter[...], grad)
        return carry

    lax.fori_loop(0, heads, body, 0, unroll=2)


def last_kernel(
    starts, base, k_ref, v_ref, gk_ref, gv_ref, z0, z1, z2, z3, grad_k, grad_v, held, leave, k_rows, v_rows
):
    heads = k_ref.shape[0]
    step, steps = pl.program_id(0), pl.num_programs(0)
    first = base[0] + step * CHUNK

    @pl.when(step == 0)
    def _():
        load_states((z0, z1, z2, z3), held)

    leave[...] = from_mask(first, last_start_to(starts, base[0] + steps * CHUNK - 1), BF16)

    def body(j, carry):
        head = own_head(base, j, heads)
        exits = held[j]
        k_rows[pl.ds(head, CHUNK, heads), :] = gk_ref[j].astype(F32) + dot_nt(v_ref[j] * leave[...], exits)
        v_rows[pl.ds(head, CHUNK, heads), :] = gv_ref[j].astype(F32) + dot_nn(k_ref[j] * leave[...], exits)
        return carry

    lax.fori_loop(0, heads, body, 0, unroll=2)
    grad_k[...] = k_rows[...].reshape(grad_k.shape).astype(BF16)
    grad_v[...] = v_rows[...].reshape(grad_v.shape).astype(BF16)


SMEM = pl.BlockSpec(memory_space=pltpu.SMEM)


def params(limit=VMEM_LIMIT):
    return pltpu.CompilerParams(dimension_semantics=("arbitrary",), vmem_limit_bytes=limit)


def whole(shape):
    return pl.BlockSpec(shape, lambda c: (0,) * len(shape))


def pair_scan(parts, backward, shard, shards, keeps, hops):
    half = len(parts) // 2
    side = lax.rem(shard, 2)
    swap = [(i, i ^ 1) for i in range(shards)]
    groups = shards // 2
    if backward:
        step = [(i, i - 2) for i in range(2, shards)]
        lead = side == 1
        lead_keep, other_keep = keeps[shard | 1], keeps[shard - side]
    else:
        step = [(i, i + 2) for i in range(shards - 2)]
        lead = side == 0
        lead_keep, other_keep = keeps[shard - side], keeps[shard | 1]
    own_out, send_out = [], []
    arrived = [lax.ppermute(p, "ctx", swap) for p in parts[half:]]
    for mine, theirs in zip(parts[:half], arrived):
        first = jnp.where(lead, mine, theirs)
        second = jnp.where(lead, theirs, mine)
        pair = second + other_keep * first
        running = pair
        incoming = None
        for hop in range(hops):
            incoming = lax.ppermute(running, "ctx", step)
            if hop + 1 < hops:
                running = pair + (other_keep * lead_keep) * incoming
        later = first + lead_keep * incoming
        own_out.append(jnp.where(lead, incoming, later))
        send_out.append(jnp.where(lead, later, incoming))
    got = [lax.ppermute(p, "ctx", swap) for p in send_out]
    return own_out + got


def sum_over(x, axis):
    size = lax.axis_size(axis)
    if size & (size - 1):
        return lax.psum(x, axis)
    distance = 1
    while distance < size:
        x = x + lax.ppermute(x, axis, [(i, i ^ distance) for i in range(size)])
        distance *= 2
    return x


def local(queries, key_rows, value_rows, grad_normed, norm_gain, document_starts):
    rows, heads, width = queries.shape
    shards = lax.axis_size("ctx")
    shard = lax.axis_index("ctx")
    features = heads * lax.axis_size("head") * width
    steps = rows // CHUNK
    part = heads // 4
    base = jnp.stack([shard * rows, lax.rem(shard, 2)]).astype(jnp.int32)
    edges = jnp.arange(shards, dtype=jnp.int32)[:, None] * rows
    inside = (document_starts[None, :] >= edges) & (document_starts[None, :] < edges + rows)
    keeps = 1.0 - jnp.any(inside, axis=1).astype(F32)

    grid = (steps,)
    native = pl.BlockSpec((CHUNK, heads, width), lambda c: (c, 0, 0))
    major = pl.BlockSpec((heads, CHUNK, width), lambda c: (0, c, 0))
    major_back = pl.BlockSpec((heads, CHUNK, width), lambda c: (0, steps - 1 - c, 0))
    state_part = whole((part, width, width))
    gain_spec = whole((heads, width))
    native_shape = jax.ShapeDtypeStruct((rows, heads, width), BF16)
    major_shape = jax.ShapeDtypeStruct((heads, rows, width), BF16)
    part_shape = jax.ShapeDtypeStruct((part, width, width), F32)
    flat_rows = pltpu.VMEM((CHUNK * heads, width), F32)
    held_bf = pltpu.VMEM((heads, width, width), BF16)
    held_f = pltpu.VMEM((heads, width, width), F32)
    token_bf = pltpu.VMEM((CHUNK, width), BF16)
    token_f = pltpu.VMEM((CHUNK, width), F32)
    mask_bf = pltpu.VMEM((CHUNK, CHUNK), BF16)
    sum_rows = 2 * rows // LANES
    sums_spec = whole((sum_rows, LANES))

    states = pl.pallas_call(
        state_kernel,
        grid=grid,
        in_specs=[SMEM, SMEM, native, native],
        out_specs=[state_part] * 4,
        out_shape=[part_shape] * 4,
        scratch_shapes=[flat_rows, flat_rows, held_f],
        compiler_params=params(),
        name="end_states",
    )(document_starts, base, key_rows, value_rows)

    entering = pair_scan(list(states), False, shard, shards, keeps, shards // 2 - 1)

    query_major, key_major, value_major, grad_major = pl.pallas_call(
        turn_kernel,
        grid=grid,
        in_specs=[SMEM] + [native] * 4,
        out_specs=[major] * 4,
        out_shape=[major_shape] * 4,
        scratch_shapes=[flat_rows] * 4,
        compiler_params=params(),
        name="head_major",
    )(base, queries, key_rows, value_rows, grad_normed)

    attended, entry = pl.pallas_call(
        local_kernel,
        grid=grid,
        in_specs=[SMEM, SMEM, major, major, major],
        out_specs=[major, pl.BlockSpec((1, heads, width, width), lambda c: (c, 0, 0, 0))],
        out_shape=[
            jax.ShapeDtypeStruct((heads, rows, width), F32),
            jax.ShapeDtypeStruct((steps, heads, width, width), BF16),
        ],
        scratch_shapes=[held_f, mask_bf, token_bf, token_bf],
        compiler_params=params(),
        name="local_attention",
    )(document_starts, base, query_major, key_major, value_major)

    sums = pl.pallas_call(
        sums_kernel,
        grid=grid,
        in_specs=[SMEM, SMEM, major, major, major, gain_spec] + [state_part] * 4,
        out_specs=sums_spec,
        out_shape=jax.ShapeDtypeStruct((sum_rows, LANES), F32),
        scratch_shapes=[held_bf, token_f, token_f, token_bf],
        compiler_params=params(),
        name="token_sums",
    )(document_starts, base, query_major, attended, grad_major, norm_gain, *entering)
    sums = lax.psum(sums, "head")

    exits = pl.pallas_call(
        functools.partial(exit_kernel, features),
        grid=grid,
        in_specs=[SMEM, SMEM, major, major, major, gain_spec, sums_spec] + [state_part] * 4,
        out_specs=[state_part] * 4,
        out_shape=[part_shape] * 4,
        scratch_shapes=[held_bf, token_f, token_f, token_bf, held_f],
        compiler_params=params(),
        name="start_grads",
    )(document_starts, base, query_major, attended, grad_major, norm_gain, sums, *entering)

    leaving = pair_scan(list(exits), True, shard, shards, keeps, shards // 2 - 1)

    normed, grad_queries, grad_att, gain_sum = pl.pallas_call(
        functools.partial(query_kernel, features),
        grid=grid,
        in_specs=[SMEM, SMEM]
        + [major] * 5
        + [pl.BlockSpec((1, heads, width, width), lambda c: (c, 0, 0, 0)), gain_spec, sums_spec]
        + [state_part] * 4,
        out_specs=[native, native, major, gain_spec],
        out_shape=[native_shape, native_shape, major_shape, jax.ShapeDtypeStruct((heads, width), F32)],
        scratch_shapes=[
            held_f, token_f, token_f, token_f, token_bf, mask_bf, flat_rows, flat_rows,
            pltpu.VMEM((heads, width), F32),
        ],
        compiler_params=params(),
        name="query_grads",
    )(
        document_starts, base, query_major, key_major, value_major, attended, grad_major, entry,
        norm_gain, sums, *entering,
    )
    grad_gain = sum_over(gain_sum, "ctx") / math.sqrt(rows * shards)

    key_local, value_local = pl.pallas_call(
        key_kernel,
        grid=grid,
        in_specs=[SMEM, SMEM] + [major_back] * 4,
        out_specs=[major_back] * 2,
        out_shape=[major_shape] * 2,
        scratch_shapes=[held_f, mask_bf, token_bf, token_bf],
        compiler_params=params(),
        name="local_key_grads",
    )(document_starts, base, query_major, key_major, value_major, grad_att)

    grad_keys, grad_values = pl.pallas_call(
        last_kernel,
        grid=grid,
        in_specs=[SMEM, SMEM] + [major] * 4 + [state_part] * 4,
        out_specs=[native] * 2,
        out_shape=[native_shape] * 2,
        scratch_shapes=[held_bf, token_bf, flat_rows, flat_rows],
        compiler_params=params(),
        name="key_grads",
    )(document_starts, base, key_major, value_major, key_local, value_local, *leaving)
    return normed, grad_queries, grad_keys, grad_values, grad_gain


def solution(mesh):
    tokens = P("ctx", "head", None)
    in_specs = (tokens, tokens, tokens, tokens, P("head", None), P())
    out_specs = (tokens, tokens, tokens, tokens, P("head", None))
    return jax.shard_map(local, mesh=mesh, in_specs=in_specs, out_specs=out_specs, check_vma=False)
```

```python
import functools
import math

import jax
import jax.numpy as jnp
from jax import lax
from jax.experimental import pallas as pl
from jax.experimental.pallas import tpu as pltpu
from jax.sharding import PartitionSpec as P

CHUNK = 256
LANES = 128
EPSILON = 1e-06
FAR = 2**30
VMEM_LIMIT = 20 * 1024 * 1024
GROUP = 16
UNROLL = 8

F32 = jnp.float32
BF16 = jnp.bfloat16


def dot_nn(a, b):
    return lax.dot_general(a, b, (((1,), (0,)), ((), ())), preferred_element_type=F32)


def dot_nt(a, b):
    return lax.dot_general(a, b, (((1,), (1,)), ((), ())), preferred_element_type=F32)


def dot_tn(a, b):
    return lax.dot_general(a, b, (((0,), (0,)), ((), ())), preferred_element_type=F32)


def first_start_from(starts, row):
    best = jnp.int32(FAR)
    for i in range(starts.shape[0]):
        best = jnp.minimum(best, jnp.where(starts[i] >= row, starts[i], FAR))
    return best


def last_start_to(starts, row):
    best = jnp.int32(0)
    for i in range(starts.shape[0]):
        best = jnp.maximum(best, jnp.where(starts[i] <= row, starts[i], 0))
    return best


def token_rows(first, shape, axis):
    return first + lax.broadcasted_iota(jnp.int32, shape, axis)


def within_mask(starts, first, axis):
    shape = (CHUNK, CHUNK)
    t = token_rows(first, shape, axis)
    s = token_rows(first, shape, 1 - axis)
    begin = jnp.zeros(shape, jnp.int32)
    for i in range(starts.shape[0]):
        begin = jnp.maximum(begin, jnp.where(starts[i] <= t, starts[i], 0))
    return jnp.where((s <= t) & (s >= begin), 1.0, 0.0).astype(BF16)


def before_mask(first, bound, dtype):
    return jnp.where(token_rows(first, (CHUNK, LANES), 0) < bound, 1.0, 0.0).astype(dtype)


def from_mask(first, bound, dtype):
    return jnp.where(token_rows(first, (CHUNK, LANES), 0) >= bound, 1.0, 0.0).astype(dtype)


def own_head(base, j, heads):
    return lax.rem(j + base[1] * (heads // 2), heads)


def to_major(block, out, first):
    for i in range(0, block.shape[0], GROUP):
        rows = pl.ds(pl.multiple_of(first + i, GROUP), GROUP)
        out[:, rows, :] = jnp.transpose(block[i : i + GROUP], (1, 0, 2))


def to_native(major, block):
    for i in range(0, block.shape[0], GROUP):
        block[i : i + GROUP] = jnp.transpose(major[:, i : i + GROUP, :], (1, 0, 2))


def chunk_rows(step):
    return pl.ds(pl.multiple_of(step * CHUNK, CHUNK), CHUNK)


def state_kernel(starts, base, k_ref, v_ref, o0, o1, o2, o3, k_major, v_major, total):
    heads = k_ref.shape[1]
    step, steps = pl.program_id(0), pl.num_programs(0)
    first = base[0] + step * CHUNK
    bound = last_start_to(starts, base[0] + steps * CHUNK - 1)
    rows = chunk_rows(step)

    @pl.when(step == 0)
    def _():
        total[...] = jnp.zeros_like(total)

    to_major(k_ref, k_major, step * CHUNK)
    to_major(v_ref, v_major, step * CHUNK)

    @pl.when(bound < first + CHUNK)
    def _():
        leave = from_mask(first, bound, BF16)
        for j in range(heads):
            head = own_head(base, j, heads)
            total[j] += dot_tn(k_major[head, rows, :] * leave, v_major[head, rows, :])

    @pl.when(step == steps - 1)
    def _():
        part = heads // 4
        for i, out in enumerate((o0, o1, o2, o3)):
            out[...] = total[i * part : (i + 1) * part]


def local_kernel(
    chunk, starts, base, q_ref, g_ref, k_major, v_major, *refs
):
    state_in = refs[1] if chunk else None
    q_major, g_major, att_ref, entry_ref, state_out, tick, mask, enter, leave = refs[2 if chunk else 1 :]
    tick[...] = jnp.zeros_like(tick)
    heads = q_ref.shape[1]
    first = base[0] + chunk * CHUNK
    rows = slice(chunk * CHUNK, (chunk + 1) * CHUNK)
    enter_end = first_start_from(starts, first)
    leave_start = last_start_to(starts, first + CHUNK - 1)
    keep = jnp.where(enter_end >= first + CHUNK, 1.0, 0.0).astype(F32)
    to_major(q_ref, q_major, 0)
    to_major(g_ref, g_major, 0)
    mask[...] = within_mask(starts, first, 0)
    enter[...] = before_mask(first, enter_end, BF16)
    leave[...] = from_mask(first, leave_start, BF16)
    for j in range(heads):
        query, key, value = q_major[j], k_major[j, rows, :], v_major[j, rows, :]
        scores = dot_nt(query, key).astype(BF16) * mask[...]
        att = dot_nn(scores, value)
        after = dot_tn(key * leave[...], value)
        if chunk:
            state = state_in[j]
            entry = state.astype(BF16)
            att += dot_nn(query * enter[...], entry)
            after += keep * state
            entry_ref[j] = entry
        else:
            entry_ref[j] = jnp.zeros(entry_ref.shape[1:], BF16)
        att_ref[j] = att
        state_out[j] = after


def load_states(parts, held):
    part = parts[0].shape[0]
    for i, ref in enumerate(parts):
        held[i * part : (i + 1) * part] = ref[...].astype(held.dtype)


def eye():
    shape = (LANES, LANES)
    return lax.broadcasted_iota(jnp.int32, shape, 0) == lax.broadcasted_iota(jnp.int32, shape, 1)


def column_of(row):
    return jnp.sum(jnp.where(eye(), row, 0.0), axis=1, keepdims=True)


def row_of(column):
    return jnp.sum(jnp.where(eye(), column, 0.0), axis=0, keepdims=True)


def sums_kernel(steps, starts, base, gain, *refs):
    q_refs, att_refs, g_refs = refs[:steps], refs[steps : 2 * steps], refs[2 * steps : 3 * steps]
    states = refs[3 * steps : 3 * steps + 4]
    att_outs = refs[3 * steps + 4 : 4 * steps + 4]
    sums, held, enter = refs[4 * steps + 4 :]
    heads = q_refs[0].shape[0]
    bound = first_start_from(starts, base[0])
    load_states(states, held)
    blocks = CHUNK // LANES
    for step in range(steps):
        q_ref, att_ref, g_ref, att_out = q_refs[step], att_refs[step], g_refs[step], att_outs[step]
        enter[...] = before_mask(base[0] + step * CHUNK, bound, BF16)
        nothing = jnp.zeros((CHUNK, LANES), F32)

        def body(j, carry, q_ref=q_ref, att_ref=att_ref, g_ref=g_ref, att_out=att_out):
            squares, cross = carry
            head = own_head(base, j, heads)
            att = att_ref[head] + dot_nn(q_ref[head] * enter[...], held[j])
            att_out[head] = att
            weighted = g_ref[head].astype(F32) * gain[pl.ds(head, 1), :]
            return squares + att * att, cross + weighted * att

        squares, cross = lax.fori_loop(0, heads, body, (nothing, nothing), unroll=UNROLL)
        for i in range(blocks):
            part = slice(i * LANES, (i + 1) * LANES)
            place = step * blocks + i
            sums[place : place + 1, :] = row_of(jnp.sum(squares[part], axis=1, keepdims=True))
            place += steps * blocks
            sums[place : place + 1, :] = row_of(jnp.sum(cross[part], axis=1, keepdims=True))


def norm_columns(sums, step, steps, features, inverse, factor):
    blocks = CHUNK // LANES

    def total(place):
        return sum(ref[place : place + 1, :] for ref in sums)

    for i in range(blocks):
        rows = slice(i * LANES, (i + 1) * LANES)
        place = step * blocks + i
        square = total(place)
        cross = total(steps * blocks + place)
        inv = 1.0 / jnp.sqrt(square / features + EPSILON)
        fac = inv * inv * inv * cross / features
        inverse[rows, :] = jnp.broadcast_to(column_of(inv), (LANES, LANES))
        factor[rows, :] = jnp.broadcast_to(column_of(fac), (LANES, LANES))


def exit_kernel(features, steps, count, starts, base, gain, *refs):
    sums, refs = refs[:count], refs[count:]
    q_refs, att_refs, g_refs = refs[:steps], refs[steps : 2 * steps], refs[2 * steps : 3 * steps]
    outs = refs[3 * steps : 3 * steps + 4]
    inverse, factor, enter, total = refs[3 * steps + 4 :]
    heads = q_refs[0].shape[0]
    bound = first_start_from(starts, base[0])
    total[...] = jnp.zeros_like(total)
    for step in range(steps):
        first = base[0] + step * CHUNK

        @pl.when(bound > first)
        def _(step=step, first=first):
            norm_columns(sums, step, steps, features, inverse, factor)
            enter[...] = before_mask(first, bound, BF16)

            def body(j, carry):
                head = own_head(base, j, heads)
                weighted = g_refs[step][head].astype(F32) * gain[pl.ds(head, 1), :]
                grad = (inverse[...] * weighted - att_refs[step][head] * factor[...]).astype(BF16)
                total[j] += dot_tn(q_refs[step][head] * enter[...], grad)
                return carry

            lax.fori_loop(0, heads, body, 0, unroll=UNROLL)

    part = heads // 4
    for i, out in enumerate(outs):
        out[...] = total[i * part : (i + 1) * part]


def query_kernel(
    features, chunk, steps, count, starts, base, k_ref, v_ref, att_ref, g_ref, entry_ref, gain, r0, r1, r2, r3, *refs
):
    sums = refs[:count]
    normed, grad_q, grad_att, gain_sum, tick = refs[-12:-7]
    held, inverse, factor, enter, mask, normed_major, grad_major = refs[-7:]
    tick[...] = jnp.zeros_like(tick)
    heads = k_ref.shape[0]
    first = base[0] + chunk * CHUNK
    rows = slice(chunk * CHUNK, (chunk + 1) * CHUNK)
    bound = first_start_from(starts, base[0])
    reach = jnp.where(bound >= first, 1.0, 0.0).astype(F32)
    load_states((r0, r1, r2, r3), held)
    norm_columns(sums, chunk, steps, features, inverse, factor)
    enter[...] = before_mask(first, first_start_from(starts, first), BF16)
    mask[...] = within_mask(starts, first, 0)
    for j in range(heads):
        head = own_head(base, j, heads)
        scale = gain[pl.ds(head, 1), :]
        att = att_ref[head]
        upstream = g_ref[head].astype(F32)
        scaled = att * inverse[...]
        normed_major[head] = (scaled * scale).astype(BF16)
        gain_sum[pl.ds(head, 1), :] = jnp.sum(upstream * scaled, axis=0, keepdims=True)
        grad = (inverse[...] * (upstream * scale) - att * factor[...]).astype(BF16)
        grad_att[head] = grad
        entry = (entry_ref[head].astype(F32) + reach * held[j]).astype(BF16)
        scores = dot_nt(grad, v_ref[head, rows, :]).astype(BF16) * mask[...]
        grad_major[head] = (
            dot_nn(scores, k_ref[head, rows, :]) + dot_nt(grad * enter[...], entry)
        ).astype(BF16)
    to_native(normed_major, normed)
    to_native(grad_major, grad_q)


def key_kernel(chunk, steps, starts, base, q_ref, k_ref, v_ref, grad_ref, *refs):
    state_in = refs[1] if chunk < steps - 1 else None
    grad_k, grad_v, state_out, tick, mask, enter, leave = refs[2 if chunk < steps - 1 else 1 :]
    tick[...] = jnp.zeros_like(tick)
    heads = q_ref.shape[0]
    first = base[0] + chunk * CHUNK
    rows = slice(chunk * CHUNK, (chunk + 1) * CHUNK)
    enter_end = first_start_from(starts, first)
    leave_start = last_start_to(starts, first + CHUNK - 1)
    keep = jnp.where(enter_end >= first + CHUNK, 1.0, 0.0).astype(F32)
    mask[...] = within_mask(starts, first, 1)
    enter[...] = before_mask(first, enter_end, BF16)
    leave[...] = from_mask(first, leave_start, BF16)
    for j in range(heads):
        query, key = q_ref[j], k_ref[j, rows, :]
        value, grad = v_ref[j, rows, :], grad_ref[j]
        scores = dot_nt(key, query).astype(BF16) * mask[...]
        value_grad = dot_nn(scores, grad)
        scores = dot_nt(value, grad).astype(BF16) * mask[...]
        key_grad = dot_nn(scores, query)
        before = dot_tn(query * enter[...], grad)
        if state_in is not None:
            state = state_in[j]
            exits = state.astype(BF16)
            value_grad += dot_nn(key * leave[...], exits)
            key_grad += dot_nt(value * leave[...], exits)
            before += keep * state
        grad_v[j] = value_grad.astype(grad_v.dtype)
        grad_k[j] = key_grad.astype(grad_k.dtype)
        state_out[j] = before


def last_kernel(steps, starts, base, k_ref, v_ref, *refs):
    gk_refs, gv_refs, states = refs[:steps], refs[steps : 2 * steps], refs[2 * steps : 2 * steps + 4]
    grad_k, grad_v, held, leave, k_rows, v_rows, k_block, v_block, sems = refs[2 * steps + 4 :]
    heads = k_ref.shape[0]
    load_states(states, held)
    bound = last_start_to(starts, base[0] + steps * CHUNK - 1)
    copies = []
    for step in range(steps):
        rows = slice(step * CHUNK, (step + 1) * CHUNK)
        leave[...] = from_mask(base[0] + step * CHUNK, bound, BF16)

        def body(j, carry, step=step, rows=rows):
            head = own_head(base, j, heads)
            exits = held[j]
            k_rows[head] = (
                gk_refs[step][head].astype(F32) + dot_nt(v_ref[head, rows, :] * leave[...], exits)
            ).astype(BF16)
            v_rows[head] = (
                gv_refs[step][head].astype(F32) + dot_nn(k_ref[head, rows, :] * leave[...], exits)
            ).astype(BF16)
            return carry

        lax.fori_loop(0, heads, body, 0, unroll=UNROLL)
        for i, (major, block, out) in enumerate(((k_rows, k_block, grad_k), (v_rows, v_block, grad_v))):
            to_native(major, block.at[step])
            copy = pltpu.make_async_copy(block.at[step], out.at[rows], sems.at[i, step])
            copy.start()
            copies.append(copy)
    for copy in copies:
        copy.wait()


SMEM = pl.BlockSpec(memory_space=pltpu.SMEM)


VMEM = pl.BlockSpec(memory_space=pltpu.VMEM)
HBM = pl.BlockSpec(memory_space=pltpu.HBM)
ANY = pl.BlockSpec(memory_space=pl.ANY)


def params(grid=True):
    order = ("arbitrary",) if grid else None
    return pltpu.CompilerParams(dimension_semantics=order, vmem_limit_bytes=VMEM_LIMIT)


def estimate():
    return pl.CostEstimate(flops=1, bytes_accessed=1, transcendentals=0)


def far(*arrays):
    return [pltpu.with_memory_space_constraint(x, pltpu.HBM) for x in arrays]


def near(*arrays):
    return [pltpu.with_memory_space_constraint(x, pltpu.VMEM) for x in arrays]


def whole(shape):
    return pl.BlockSpec(shape, lambda c: (0,) * len(shape))


def keep_of(starts, row, rows):
    return jnp.where(first_start_from(starts, row) >= row + rows, 1.0, 0.0).astype(F32)


def pair_keeps(starts, base, rows, backward):
    side = base[1]
    row = base[0] - side * rows
    low, high = keep_of(starts, row, rows), keep_of(starts, row + rows, rows)
    if backward:
        return side == 1, high, low
    return side == 0, low, high


def pair_kernel(rows, backward, starts, base, mine, theirs, tick, first, pair):
    lead, _, second_keep = pair_keeps(starts, base, rows, backward)
    first[...] = jnp.where(lead, mine[...], theirs[...])
    pair[...] = jnp.where(lead, theirs[...], mine[...]) + second_keep * first[...]


def hop_kernel(rows, backward, starts, base, pair, moved, tick, out):
    _, first_keep, second_keep = pair_keeps(starts, base, rows, backward)
    out[...] = pair[...] + (first_keep * second_keep) * moved[...]


def split_kernel(rows, backward, starts, base, first, moved, tick, own, other):
    lead, first_keep, _ = pair_keeps(starts, base, rows, backward)
    early = moved[...]
    late = first[...] + first_keep * early
    own[...] = jnp.where(lead, early, late)
    other[...] = jnp.where(lead, late, early)


def small_call(kernel, name, count, starts, base, *arrays):
    shape = jax.ShapeDtypeStruct(arrays[0].shape, F32)
    return pl.pallas_call(
        kernel,
        in_specs=[SMEM, SMEM, VMEM, VMEM, ANY],
        out_specs=[VMEM] * count,
        out_shape=[shape] * count,
        compiler_params=pltpu.CompilerParams(vmem_limit_bytes=8 * 1024 * 1024),
        cost_estimate=estimate(),
        name=name,
    )(starts, base, *arrays)


def pair_scan(parts, backward, scalars, rows, hops, works):
    half = len(parts) // 2
    works = list(works)
    shards = lax.axis_size("ctx")
    swap = [(i, i ^ 1) for i in range(shards)]
    if backward:
        step = [(i, i - 2) for i in range(2, shards)]
    else:
        step = [(i, i + 2) for i in range(shards - 2)]

    def work(after):
        return works.pop(0)(after) if works else after

    def call(kernel, name, count, *arrays):
        return small_call(functools.partial(kernel, rows, backward), name, count, *scalars, *arrays)

    arrived = [lax.ppermute(p, "ctx", swap) for p in parts[half:]]
    after = parts[half]
    firsts, pairs, moved = [], [], []
    for mine, theirs in zip(parts[:half], arrived):
        first, pair = call(pair_kernel, "pair_states", 2, mine, theirs, work(after))
        firsts.append(first)
        pairs.append(pair)
        moved.append(lax.ppermute(pair, "ctx", step))
        after = pair
    for _ in range(1, hops):
        for i, pair in enumerate(pairs):
            (after,) = call(hop_kernel, "chain_states", 1, pair, moved[i], work(after))
            moved[i] = lax.ppermute(after, "ctx", step)
    own_out, got = [], []
    for first, incoming in zip(firsts, moved):
        own, after = call(split_kernel, "split_states", 2, first, incoming, work(after))
        own_out.append(own)
        got.append(lax.ppermute(after, "ctx", swap))
    while works:
        work(after)
    return own_out + got


def sum_over(x, axis):
    size = lax.axis_size(axis)
    if size & (size - 1):
        return lax.psum(x, axis)
    distance = 1
    while distance < size:
        x = x + lax.ppermute(x, axis, [(i, i ^ distance) for i in range(size)])
        distance *= 2
    return x


def from_all(x, axis):
    size = lax.axis_size(axis)
    return [x] + [
        lax.ppermute(x, axis, [(i, (i + d) % size) for i in range(size)]) for d in range(1, size)
    ]


def local(queries, key_rows, value_rows, grad_normed, norm_gain, document_starts):
    rows, heads, width = queries.shape
    shards = lax.axis_size("ctx")
    shard = lax.axis_index("ctx")
    features = heads * lax.axis_size("head") * width
    steps = rows // CHUNK
    part = heads // 4
    base = jnp.stack([shard * rows, lax.rem(shard, 2)]).astype(jnp.int32)
    hops = shards // 2 - 1

    native = pl.BlockSpec((CHUNK, heads, width), lambda c: (c, 0, 0))
    native_shape = jax.ShapeDtypeStruct((rows, heads, width), BF16)
    major_shape = pltpu.VMEM((heads, rows, width), BF16)
    chunk_shape = pltpu.VMEM((heads, CHUNK, width), BF16)
    chunk_wide = pltpu.VMEM((heads, CHUNK, width), F32)
    part_spec = pl.BlockSpec((part, width, width), lambda c: (0, 0, 0))
    part_shape = jax.ShapeDtypeStruct((part, width, width), F32)
    held_bf = pltpu.VMEM((heads, width, width), BF16)
    held_f = pltpu.VMEM((heads, width, width), F32)
    token_bf = pltpu.VMEM((CHUNK, width), BF16)
    token_f = pltpu.VMEM((CHUNK, width), F32)
    mask_bf = pltpu.VMEM((CHUNK, CHUNK), BF16)
    sum_rows = 2 * rows // LANES
    sums_shape = jax.ShapeDtypeStruct((sum_rows, LANES), F32)
    gain_shape = jax.ShapeDtypeStruct((heads, width), F32)
    tick_shape = jax.ShapeDtypeStruct((8, LANES), F32)
    scalars = (document_starts, base)

    *states, key_major, value_major = pl.pallas_call(
        state_kernel,
        grid=(steps,),
        in_specs=[SMEM, SMEM, native, native],
        out_specs=[part_spec] * 4 + [VMEM] * 2,
        out_shape=[part_shape] * 4 + [major_shape] * 2,
        scratch_shapes=[held_f],
        compiler_params=params(),
        cost_estimate=estimate(),
        name="end_states",
    )(*scalars, *far(key_rows, value_rows))

    query, grad, attended, entry = [], [], [], []
    state = []

    def local_work(c, after):
        block = pl.BlockSpec((CHUNK, heads, width), lambda i: (c, 0, 0))
        *made, next_state, tick = pl.pallas_call(
            functools.partial(local_kernel, c),
            grid=(1,),
            in_specs=[SMEM, SMEM, block, block, VMEM, VMEM, ANY] + [VMEM] * min(c, 1),
            out_specs=[VMEM] * 6,
            out_shape=[chunk_shape, chunk_shape, chunk_wide, held_bf, held_f, tick_shape],
            scratch_shapes=[mask_bf, token_bf, token_bf],
            compiler_params=params(),
            cost_estimate=estimate(),
            name="local_attention",
        )(*scalars, *far(queries, grad_normed), *near(key_major, value_major), after, *near(*state))
        for kept, one in zip((query, grad, attended, entry), made):
            kept.append(one)
        state[:] = [next_state]
        return tick

    entering = pair_scan(
        list(states), False, scalars, rows, hops,
        [functools.partial(local_work, c) for c in range(steps)],
    )

    *attended, sums = pl.pallas_call(
        functools.partial(sums_kernel, steps),
        in_specs=[SMEM, SMEM] + [VMEM] * (3 * steps + 5),
        out_specs=[VMEM] * (steps + 1),
        out_shape=[chunk_wide] * steps + [sums_shape],
        scratch_shapes=[held_bf, token_bf],
        input_output_aliases={3 + steps + c: c for c in range(steps)},
        compiler_params=params(False),
        cost_estimate=estimate(),
        name="token_sums",
    )(*scalars, norm_gain, *near(*query, *attended, *grad), *entering)
    sums = from_all(sums, "head")

    exits = pl.pallas_call(
        functools.partial(exit_kernel, features, steps, len(sums)),
        in_specs=[SMEM, SMEM] + [VMEM] * (3 * steps + 1 + len(sums)),
        out_specs=[VMEM] * 4,
        out_shape=[part_shape] * 4,
        scratch_shapes=[token_f, token_f, token_bf, held_f],
        compiler_params=params(False),
        cost_estimate=estimate(),
        name="start_grads",
    )(*scalars, norm_gain, *sums, *near(*query, *attended, *grad))

    natives, gain_parts, grad_att = [], [], [None]
    key_local, value_local = [None] * steps, [None] * steps
    exit_state = []

    def query_work(c, after):
        block = pl.BlockSpec((CHUNK, heads, width), lambda i: (c, 0, 0))
        *outs, grad_att[0], gain_part, tick = pl.pallas_call(
            functools.partial(query_kernel, features, c, steps, len(sums)),
            grid=(1,),
            in_specs=[SMEM, SMEM] + [VMEM] * (10 + len(sums)) + [ANY] + [HBM] * len(natives),
            out_specs=[block, block, VMEM, VMEM, VMEM],
            out_shape=[native_shape, native_shape, chunk_shape, gain_shape, tick_shape],
            scratch_shapes=[held_f, token_f, token_f, token_bf, mask_bf, chunk_shape, chunk_shape],
            input_output_aliases={13 + len(sums) + i: i for i in range(len(natives))},
            compiler_params=params(),
            cost_estimate=estimate(),
            name="query_grads",
        )(
            *scalars, *near(key_major, value_major, attended[c], grad[c], entry[c]),
            norm_gain, *entering, *sums, after, *natives,
        )
        gain_parts.append(gain_part)
        natives[:] = outs
        return tick

    def key_work(c, after):
        key_local[c], value_local[c], next_state, tick = pl.pallas_call(
            functools.partial(key_kernel, c, steps),
            in_specs=[SMEM, SMEM] + [VMEM] * 4 + [ANY] + [VMEM] * len(exit_state),
            out_specs=[VMEM] * 4,
            out_shape=[chunk_shape, chunk_shape, held_f, tick_shape],
            scratch_shapes=[mask_bf, token_bf, token_bf],
            compiler_params=params(False),
            cost_estimate=estimate(),
            name="local_key_grads",
        )(*scalars, *near(query[c], key_major, value_major, grad_att[0]), after, *near(*exit_state))
        exit_state[:] = [next_state]
        return tick

    works = []
    for c in reversed(range(steps)):
        works += [functools.partial(query_work, c), functools.partial(key_work, c)]
    leaving = pair_scan(list(exits), True, scalars, rows, hops, works)
    normed, grad_queries = natives
    grad_gain = sum_over(sum(gain_parts), "ctx") / math.sqrt(rows * shards)

    grad_keys, grad_values = pl.pallas_call(
        functools.partial(last_kernel, steps),
        in_specs=[SMEM, SMEM] + [VMEM] * (2 * steps + 6),
        out_specs=[HBM] * 2,
        out_shape=[native_shape] * 2,
        scratch_shapes=[
            held_bf, token_bf, chunk_shape, chunk_shape,
            pltpu.VMEM((steps, CHUNK, heads, width), BF16),
            pltpu.VMEM((steps, CHUNK, heads, width), BF16),
            pltpu.SemaphoreType.DMA((2, steps)),
        ],
        compiler_params=params(False),
        cost_estimate=estimate(),
        name="key_grads",
    )(*scalars, *near(key_major, value_major, *key_local, *value_local), *leaving)
    return normed, grad_queries, grad_keys, grad_values, grad_gain


def solution(mesh):
    tokens = P("ctx", "head", None)
    in_specs = (tokens, tokens, tokens, tokens, P("head", None), P())
    out_specs = (tokens, tokens, tokens, tokens, P("head", None))
    return jax.shard_map(local, mesh=mesh, in_specs=in_specs, out_specs=out_specs, check_vma=False)
```

```python
import functools
import math

import jax
import jax.numpy as jnp
from jax import lax
from jax.experimental import pallas as pl
from jax.experimental.pallas import tpu as pltpu
from jax.sharding import PartitionSpec as P

CHUNK = 256
LANES = 128
EPSILON = 1e-06
FAR = 2**30
VMEM_LIMIT = 20 * 1024 * 1024
GROUP = 16
UNROLL = 8

F32 = jnp.float32
BF16 = jnp.bfloat16


def dot_nn(a, b):
    return lax.dot_general(a, b, (((1,), (0,)), ((), ())), preferred_element_type=F32)


def dot_nt(a, b):
    return lax.dot_general(a, b, (((1,), (1,)), ((), ())), preferred_element_type=F32)


def dot_tn(a, b):
    return lax.dot_general(a, b, (((0,), (0,)), ((), ())), preferred_element_type=F32)


def block_diagonal(a, b):
    nothing = jnp.zeros_like(a)
    return jnp.concatenate(
        [jnp.concatenate([a, nothing], axis=1), jnp.concatenate([nothing, b], axis=1)], axis=0
    )


def side_by_side(a, b):
    return jnp.concatenate([a, b], axis=1)


def first_start_from(starts, row):
    best = jnp.int32(FAR)
    for i in range(starts.shape[0]):
        best = jnp.minimum(best, jnp.where(starts[i] >= row, starts[i], FAR))
    return best


def last_start_to(starts, row):
    best = jnp.int32(0)
    for i in range(starts.shape[0]):
        best = jnp.maximum(best, jnp.where(starts[i] <= row, starts[i], 0))
    return best


def token_rows(first, shape, axis):
    return first + lax.broadcasted_iota(jnp.int32, shape, axis)


def within_mask(starts, first, axis):
    shape = (CHUNK, CHUNK)
    t = token_rows(first, shape, axis)
    s = token_rows(first, shape, 1 - axis)
    begin = jnp.zeros(shape, jnp.int32)
    for i in range(starts.shape[0]):
        begin = jnp.maximum(begin, jnp.where(starts[i] <= t, starts[i], 0))
    return jnp.where((s <= t) & (s >= begin), 1.0, 0.0).astype(BF16)


def before_mask(first, bound, dtype):
    return jnp.where(token_rows(first, (CHUNK, LANES), 0) < bound, 1.0, 0.0).astype(dtype)


def from_mask(first, bound, dtype):
    return jnp.where(token_rows(first, (CHUNK, LANES), 0) >= bound, 1.0, 0.0).astype(dtype)


def own_head(base, j, heads):
    return lax.rem(j + base[1] * (heads // 2), heads)


def to_major(block, out, first):
    for i in range(0, block.shape[0], GROUP):
        rows = pl.ds(pl.multiple_of(first + i, GROUP), GROUP)
        out[:, rows, :] = jnp.transpose(block[i : i + GROUP], (1, 0, 2))


def to_native(major, block):
    for i in range(0, block.shape[0], GROUP):
        block[i : i + GROUP] = jnp.transpose(major[:, i : i + GROUP, :], (1, 0, 2))


def chunk_rows(step):
    return pl.ds(pl.multiple_of(step * CHUNK, CHUNK), CHUNK)


def state_kernel(starts, base, k_ref, v_ref, o0, o1, o2, o3, k_major, v_major, total):
    heads = k_ref.shape[1]
    step, steps = pl.program_id(0), pl.num_programs(0)
    first = base[0] + step * CHUNK
    bound = last_start_to(starts, base[0] + steps * CHUNK - 1)
    rows = chunk_rows(step)

    @pl.when(step == 0)
    def _():
        total[...] = jnp.zeros_like(total)

    to_major(k_ref, k_major, step * CHUNK)
    to_major(v_ref, v_major, step * CHUNK)

    @pl.when(bound < first + CHUNK)
    def _():
        leave = from_mask(first, bound, BF16)
        for j in range(heads):
            head = own_head(base, j, heads)
            total[j] += dot_tn(k_major[head, rows, :] * leave, v_major[head, rows, :])

    @pl.when(step == steps - 1)
    def _():
        part = heads // 4
        for i, out in enumerate((o0, o1, o2, o3)):
            out[...] = total[i * part : (i + 1) * part]


def local_kernel(
    chunk, starts, base, q_ref, g_ref, k_major, v_major, *refs
):
    state_in = refs[1] if chunk else None
    q_major, g_major, att_ref, entry_ref, q_turned, state_out, tick, mask, enter, leave, reach = refs[2 if chunk else 1 :]
    tick[...] = jnp.zeros_like(tick)
    heads, width = q_ref.shape[1:]
    first = base[0] + chunk * CHUNK
    rows = slice(chunk * CHUNK, (chunk + 1) * CHUNK)
    enter_end = first_start_from(starts, first)
    leave_start = last_start_to(starts, first + CHUNK - 1)
    keep = jnp.where(enter_end >= first + CHUNK, 1.0, 0.0).astype(F32)
    to_major(q_ref, q_major, 0)
    to_major(g_ref, g_major, 0)
    reach[...] = before_mask(first, first_start_from(starts, base[0]), BF16)
    mask[...] = within_mask(starts, first, 0)
    enter[...] = before_mask(first, enter_end, BF16)
    leave[...] = from_mask(first, leave_start, BF16)
    for p in range(0, heads, 2):
        pair = (p, p + 1)
        if chunk:
            entry = [state_in[j].astype(BF16) for j in pair]
            inter = dot_nn(
                side_by_side(*[q_major[j] * enter[...] for j in pair]), block_diagonal(*entry)
            )
        for i, j in enumerate(pair):
            query, key, value = q_major[j], k_major[j, rows, :], v_major[j, rows, :]
            scores = dot_nt(query, key).astype(BF16) * mask[...]
            att = dot_nn(scores, value)
            q_turned[j] = jnp.transpose(query * reach[...], (1, 0))
            after = dot_tn(key * leave[...], value)
            if chunk:
                att += inter[:, i * width : (i + 1) * width]
                after += keep * state_in[j]
                entry_ref[j] = entry[i]
            else:
                entry_ref[j] = jnp.zeros(entry_ref.shape[1:], BF16)
            att_ref[j] = att
            state_out[j] = after


def load_states(parts, held):
    part = parts[0].shape[0]
    for i, ref in enumerate(parts):
        held[i * part : (i + 1) * part] = ref[...].astype(held.dtype)


def eye():
    shape = (LANES, LANES)
    return lax.broadcasted_iota(jnp.int32, shape, 0) == lax.broadcasted_iota(jnp.int32, shape, 1)


def column_of(row):
    return jnp.sum(jnp.where(eye(), row, 0.0), axis=1, keepdims=True)


def row_of(column):
    return jnp.sum(jnp.where(eye(), column, 0.0), axis=0, keepdims=True)


def sums_kernel(steps, starts, base, gain, *refs):
    q_refs, att_refs, g_refs = refs[:steps], refs[steps : 2 * steps], refs[2 * steps : 3 * steps]
    states = refs[3 * steps : 3 * steps + 4]
    att_outs = refs[3 * steps + 4 : 4 * steps + 4]
    sums, held, enter = refs[4 * steps + 4 :]
    heads = q_refs[0].shape[0]
    bound = first_start_from(starts, base[0])
    load_states(states, held)
    blocks = CHUNK // LANES
    for step in range(steps):
        q_ref, att_ref, g_ref, att_out = q_refs[step], att_refs[step], g_refs[step], att_outs[step]
        enter[...] = before_mask(base[0] + step * CHUNK, bound, BF16)
        nothing = jnp.zeros((CHUNK, LANES), F32)

        def body(p, carry, q_ref=q_ref, att_ref=att_ref, g_ref=g_ref, att_out=att_out):
            squares, cross = carry
            places = [2 * p, 2 * p + 1]
            own = [own_head(base, j, heads) for j in places]
            inter = dot_nn(
                side_by_side(*[q_ref[head] * enter[...] for head in own]),
                block_diagonal(*[held[j] for j in places]),
            )
            for i, head in enumerate(own):
                att = att_ref[head] + inter[:, i * LANES : (i + 1) * LANES]
                att_out[head] = att
                weighted = g_ref[head].astype(F32) * gain[pl.ds(head, 1), :]
                squares = squares + att * att
                cross = cross + weighted * att
            return squares, cross

        squares, cross = lax.fori_loop(0, heads // 2, body, (nothing, nothing), unroll=UNROLL // 2)
        for i in range(blocks):
            part = slice(i * LANES, (i + 1) * LANES)
            place = step * blocks + i
            sums[place : place + 1, :] = row_of(jnp.sum(squares[part], axis=1, keepdims=True))
            place += steps * blocks
            sums[place : place + 1, :] = row_of(jnp.sum(cross[part], axis=1, keepdims=True))


def norm_columns(sums, step, steps, features, inverse, factor):
    blocks = CHUNK // LANES

    def total(place):
        return sum(ref[place : place + 1, :] for ref in sums)

    for i in range(blocks):
        rows = slice(i * LANES, (i + 1) * LANES)
        place = step * blocks + i
        square = total(place)
        cross = total(steps * blocks + place)
        inv = 1.0 / jnp.sqrt(square / features + EPSILON)
        fac = inv * inv * inv * cross / features
        inverse[rows, :] = jnp.broadcast_to(column_of(inv), (LANES, LANES))
        factor[rows, :] = jnp.broadcast_to(column_of(fac), (LANES, LANES))


def exit_kernel(features, steps, count, starts, base, gain, *refs):
    sums, refs = refs[:count], refs[count:]
    q_refs, att_refs, g_refs = refs[:steps], refs[steps : 2 * steps], refs[2 * steps : 3 * steps]
    outs = refs[3 * steps : 3 * steps + 4]
    gain_sum, inverse, factor, total = refs[3 * steps + 4 :]
    heads = q_refs[0].shape[0]
    total[...] = jnp.zeros_like(total)
    gain_sum[...] = jnp.zeros_like(gain_sum)
    for step in range(steps):
        norm_columns(sums, step, steps, features, inverse, factor)

        def body(j, carry, step=step):
            head = own_head(base, j, heads)
            upstream = g_refs[step][head].astype(F32)
            att = att_refs[step][head]
            scaled = inverse[...] * upstream
            gain_sum[pl.ds(head, 1), :] += jnp.sum(scaled * att, axis=0, keepdims=True)
            grad = (scaled * gain[pl.ds(head, 1), :] - att * factor[...]).astype(BF16)
            total[j] += dot_nn(q_refs[step][head], grad)
            return carry

        lax.fori_loop(0, heads, body, 0, unroll=UNROLL)

    part = heads // 4
    for i, out in enumerate(outs):
        out[...] = total[i * part : (i + 1) * part]


def grad_kernel(
    features, chunk, steps, count, starts, base, q_ref, k_ref, v_ref, att_ref, g_ref, entry_ref, gain,
    r0, r1, r2, r3, *refs
):
    sums, refs = refs[:count], refs[count:]
    state_in = refs[2] if chunk < steps - 1 else None
    normed, grad_q, grad_k, grad_v, state_out, tick = refs[-14:-8]
    held, inverse, factor, enter, leave, masks, normed_major, grad_major = refs[-8:]
    tick[...] = jnp.zeros_like(tick)
    heads, _, width = q_ref.shape
    first = base[0] + chunk * CHUNK
    rows = slice(chunk * CHUNK, (chunk + 1) * CHUNK)
    bound = first_start_from(starts, base[0])
    reach = jnp.where(bound >= first, 1.0, 0.0).astype(F32)
    enter_end = first_start_from(starts, first)
    leave_start = last_start_to(starts, first + CHUNK - 1)
    keep = jnp.where(enter_end >= first + CHUNK, 1.0, 0.0).astype(F32)
    load_states((r0, r1, r2, r3), held)
    norm_columns(sums, chunk, steps, features, inverse, factor)
    enter[...] = before_mask(first, enter_end, BF16)
    leave[...] = from_mask(first, leave_start, BF16)
    masks[0] = within_mask(starts, first, 0)
    masks[1] = within_mask(starts, first, 1)
    for p in range(0, heads, 2):
        places = (p, p + 1)
        own = [own_head(base, j, heads) for j in places]
        grads, entries = [], []
        for j, head in zip(places, own):
            scale = gain[pl.ds(head, 1), :]
            att = att_ref[head]
            scaled = att * inverse[...]
            normed_major[head] = (scaled * scale).astype(BF16)
            weighted = g_ref[head].astype(F32) * scale
            grads.append((inverse[...] * weighted - att * factor[...]).astype(BF16))
            entries.append((entry_ref[head].astype(F32) + reach * held[j]).astype(BF16))
        inter = dot_nt(
            side_by_side(*[grad * enter[...] for grad in grads]), block_diagonal(*entries)
        )
        if state_in is not None:
            exits = block_diagonal(*[state_in[head].astype(BF16) for head in own])
            key_inter = dot_nt(side_by_side(*[v_ref[head, rows, :] * leave[...] for head in own]), exits)
            value_inter = dot_nn(side_by_side(*[k_ref[head, rows, :] * leave[...] for head in own]), exits)
        for i, (head, grad) in enumerate(zip(own, grads)):
            lanes = slice(i * width, (i + 1) * width)
            query, key, value = q_ref[head], k_ref[head, rows, :], v_ref[head, rows, :]
            scores = dot_nt(grad, value).astype(BF16) * masks[0]
            grad_major[head] = (dot_nn(scores, key) + inter[:, lanes]).astype(BF16)
            key_grad = dot_tn(scores, query)
            scores = dot_nt(key, query).astype(BF16) * masks[1]
            value_grad = dot_nn(scores, grad)
            before = dot_tn(query * enter[...], grad)
            if state_in is not None:
                key_grad += key_inter[:, lanes]
                value_grad += value_inter[:, lanes]
                before += keep * state_in[head]
            grad_k[head] = key_grad.astype(BF16)
            grad_v[head] = value_grad.astype(BF16)
            state_out[head] = before
    to_native(normed_major, normed)
    to_native(grad_major, grad_q)


def last_kernel(steps, starts, base, k_ref, v_ref, *refs):
    gk_refs, gv_refs, states = refs[:steps], refs[steps : 2 * steps], refs[2 * steps : 2 * steps + 4]
    grad_k, grad_v, held, leave, k_rows, v_rows, k_block, v_block, sems = refs[2 * steps + 4 :]
    heads, _, width = k_ref.shape
    load_states(states, held)
    bound = last_start_to(starts, base[0] + steps * CHUNK - 1)
    copies = []
    for step in range(steps):
        rows = slice(step * CHUNK, (step + 1) * CHUNK)
        leave[...] = from_mask(base[0] + step * CHUNK, bound, BF16)

        def body(p, carry, step=step, rows=rows):
            places = (2 * p, 2 * p + 1)
            own = [own_head(base, j, heads) for j in places]
            exits = block_diagonal(*[held[j] for j in places])
            key_inter = dot_nt(side_by_side(*[v_ref[head, rows, :] * leave[...] for head in own]), exits)
            value_inter = dot_nn(side_by_side(*[k_ref[head, rows, :] * leave[...] for head in own]), exits)
            for i, head in enumerate(own):
                lanes = slice(i * width, (i + 1) * width)
                k_rows[head] = (gk_refs[step][head].astype(F32) + key_inter[:, lanes]).astype(BF16)
                v_rows[head] = (gv_refs[step][head].astype(F32) + value_inter[:, lanes]).astype(BF16)
            return carry

        lax.fori_loop(0, heads // 2, body, 0, unroll=UNROLL // 2)
        for i, (major, block, out) in enumerate(((k_rows, k_block, grad_k), (v_rows, v_block, grad_v))):
            to_native(major, block.at[step])
            copy = pltpu.make_async_copy(block.at[step], out.at[rows], sems.at[i, step])
            copy.start()
            copies.append(copy)
    for copy in copies:
        copy.wait()


SMEM = pl.BlockSpec(memory_space=pltpu.SMEM)


VMEM = pl.BlockSpec(memory_space=pltpu.VMEM)
HBM = pl.BlockSpec(memory_space=pltpu.HBM)
ANY = pl.BlockSpec(memory_space=pl.ANY)


def params(grid=True):
    order = ("arbitrary",) if grid else None
    return pltpu.CompilerParams(dimension_semantics=order, vmem_limit_bytes=VMEM_LIMIT)


def estimate():
    return pl.CostEstimate(flops=1, bytes_accessed=1, transcendentals=0)


def far(*arrays):
    return [pltpu.with_memory_space_constraint(x, pltpu.HBM) for x in arrays]


def near(*arrays):
    return [pltpu.with_memory_space_constraint(x, pltpu.VMEM) for x in arrays]


def whole(shape):
    return pl.BlockSpec(shape, lambda c: (0,) * len(shape))


def keep_of(starts, row, rows):
    return jnp.where(first_start_from(starts, row) >= row + rows, 1.0, 0.0).astype(F32)


def pair_keeps(starts, base, rows, backward):
    side = base[1]
    row = base[0] - side * rows
    low, high = keep_of(starts, row, rows), keep_of(starts, row + rows, rows)
    if backward:
        return side == 1, high, low
    return side == 0, low, high


def pair_kernel(rows, backward, starts, base, mine, theirs, tick, first, pair):
    lead, _, second_keep = pair_keeps(starts, base, rows, backward)
    first[...] = jnp.where(lead, mine[...], theirs[...])
    pair[...] = jnp.where(lead, theirs[...], mine[...]) + second_keep * first[...]


def hop_kernel(rows, backward, starts, base, pair, moved, tick, out):
    _, first_keep, second_keep = pair_keeps(starts, base, rows, backward)
    out[...] = pair[...] + (first_keep * second_keep) * moved[...]


def split_kernel(rows, backward, starts, base, first, moved, tick, own, other):
    lead, first_keep, _ = pair_keeps(starts, base, rows, backward)
    early = moved[...]
    late = first[...] + first_keep * early
    own[...] = jnp.where(lead, early, late)
    other[...] = jnp.where(lead, late, early)


def small_call(kernel, name, count, starts, base, *arrays):
    shape = jax.ShapeDtypeStruct(arrays[0].shape, F32)
    return pl.pallas_call(
        kernel,
        in_specs=[SMEM, SMEM, VMEM, VMEM, ANY],
        out_specs=[VMEM] * count,
        out_shape=[shape] * count,
        compiler_params=pltpu.CompilerParams(vmem_limit_bytes=8 * 1024 * 1024),
        cost_estimate=estimate(),
        name=name,
    )(starts, base, *arrays)


def pair_scan(parts, backward, scalars, rows, hops, works):
    half = len(parts) // 2
    works = list(works)
    shards = lax.axis_size("ctx")
    swap = [(i, i ^ 1) for i in range(shards)]
    if backward:
        step = [(i, i - 2) for i in range(2, shards)]
    else:
        step = [(i, i + 2) for i in range(shards - 2)]

    def work(i, after):
        return works.pop(0)(after) if works and (i == half - 1 or not firsts) else after

    def call(kernel, name, count, *arrays):
        return small_call(functools.partial(kernel, rows, backward), name, count, *scalars, *arrays)

    arrived = [lax.ppermute(p, "ctx", swap) for p in parts[half:]]
    after = parts[half]
    firsts, pairs, moved = [], [], []
    for i, (mine, theirs) in enumerate(zip(parts[:half], arrived)):
        first, pair = call(pair_kernel, "pair_states", 2, mine, theirs, work(i, after))
        firsts.append(first)
        pairs.append(pair)
        moved.append(lax.ppermute(pair, "ctx", step))
        after = pair
    for _ in range(1, hops):
        for i, pair in enumerate(pairs):
            (after,) = call(hop_kernel, "chain_states", 1, pair, moved[i], work(i, after))
            moved[i] = lax.ppermute(after, "ctx", step)
    own_out, got = [], []
    for i, (first, incoming) in enumerate(zip(firsts, moved)):
        own, after = call(split_kernel, "split_states", 2, first, incoming, work(i, after))
        own_out.append(own)
        got.append(lax.ppermute(after, "ctx", swap))
    while works:
        work(half - 1, after)
    return own_out + got


def add_kernel(a, b, tick, out):
    out[...] = a[...] + b[...]


class SwapSum:
    def __init__(self, x, axis):
        self.x, self.axis, self.size, self.distance = x, axis, lax.axis_size(axis), 1
        self.swap()

    def swap(self):
        pairs = [(i, i ^ self.distance) for i in range(self.size)]
        self.moved = lax.ppermute(self.x, self.axis, pairs) if self.distance < self.size else None

    def step(self, after):
        if self.moved is None:
            return
        self.x = pl.pallas_call(
            add_kernel,
            in_specs=[VMEM, VMEM, ANY],
            out_specs=VMEM,
            out_shape=jax.ShapeDtypeStruct(self.x.shape, F32),
            compiler_params=pltpu.CompilerParams(vmem_limit_bytes=8 * 1024 * 1024),
            cost_estimate=estimate(),
            name="gain_sum",
        )(self.x, self.moved, after)
        self.distance *= 2
        self.swap()

    def result(self, after):
        while self.moved is not None:
            self.step(after)
        return self.x


def from_all(x, axis):
    size = lax.axis_size(axis)
    return [x] + [
        lax.ppermute(x, axis, [(i, (i + d) % size) for i in range(size)]) for d in range(1, size)
    ]


def pairs_crossed(document_starts, rows, shards):
    ends = jnp.concatenate([document_starts[1:], jnp.full((1,), shards * rows, jnp.int32)])
    return jnp.max(lax.div(ends - 1, 2 * rows) - lax.div(document_starts, 2 * rows))


def local(*args):
    rows, document_starts = args[0].shape[0], args[-1]
    shards = lax.axis_size("ctx")
    most = shards // 2 - 1
    counts = sorted({min(1, most), min(2, most), most})
    crossed = pairs_crossed(document_starts, rows, shards)
    index = sum((crossed > count).astype(jnp.int32) for count in counts[:-1])
    return lax.switch(index, [functools.partial(with_hops, count) for count in counts], *args)


def with_hops(hops, queries, key_rows, value_rows, grad_normed, norm_gain, document_starts):
    rows, heads, width = queries.shape
    shards = lax.axis_size("ctx")
    shard = lax.axis_index("ctx")
    features = heads * lax.axis_size("head") * width
    steps = rows // CHUNK
    part = heads // 4
    base = jnp.stack([shard * rows, lax.rem(shard, 2)]).astype(jnp.int32)

    native = pl.BlockSpec((CHUNK, heads, width), lambda c: (c, 0, 0))
    native_shape = jax.ShapeDtypeStruct((rows, heads, width), BF16)
    major_shape = pltpu.VMEM((heads, rows, width), BF16)
    chunk_shape = pltpu.VMEM((heads, CHUNK, width), BF16)
    turned_shape = pltpu.VMEM((heads, width, CHUNK), BF16)
    chunk_wide = pltpu.VMEM((heads, CHUNK, width), F32)
    part_spec = pl.BlockSpec((part, width, width), lambda c: (0, 0, 0))
    part_shape = jax.ShapeDtypeStruct((part, width, width), F32)
    held_bf = pltpu.VMEM((heads, width, width), BF16)
    held_f = pltpu.VMEM((heads, width, width), F32)
    token_bf = pltpu.VMEM((CHUNK, width), BF16)
    token_f = pltpu.VMEM((CHUNK, width), F32)
    mask_bf = pltpu.VMEM((CHUNK, CHUNK), BF16)
    sum_rows = 2 * rows // LANES
    sums_shape = jax.ShapeDtypeStruct((sum_rows, LANES), F32)
    gain_shape = jax.ShapeDtypeStruct((heads, width), F32)
    tick_shape = jax.ShapeDtypeStruct((8, LANES), F32)
    scalars = (document_starts, base)

    *states, key_major, value_major = pl.pallas_call(
        state_kernel,
        grid=(steps,),
        in_specs=[SMEM, SMEM, native, native],
        out_specs=[part_spec] * 4 + [VMEM] * 2,
        out_shape=[part_shape] * 4 + [major_shape] * 2,
        scratch_shapes=[held_f],
        compiler_params=params(),
        cost_estimate=estimate(),
        name="end_states",
    )(*scalars, *far(key_rows, value_rows))

    query, grad, attended, entry, turned = [], [], [], [], []
    state = []

    def local_work(c, after):
        block = pl.BlockSpec((CHUNK, heads, width), lambda i: (c, 0, 0))
        *made, next_state, tick = pl.pallas_call(
            functools.partial(local_kernel, c),
            grid=(1,),
            in_specs=[SMEM, SMEM, block, block, VMEM, VMEM, ANY] + [VMEM] * min(c, 1),
            out_specs=[VMEM] * 7,
            out_shape=[chunk_shape, chunk_shape, chunk_wide, held_bf, turned_shape, held_f, tick_shape],
            scratch_shapes=[mask_bf, token_bf, token_bf, token_bf],
            compiler_params=params(),
            cost_estimate=estimate(),
            name="local_attention",
        )(*scalars, *far(queries, grad_normed), *near(key_major, value_major), after, *near(*state))
        for kept, one in zip((query, grad, attended, entry, turned), made):
            kept.append(one)
        state[:] = [next_state]
        return tick

    entering = pair_scan(
        list(states), False, scalars, rows, hops,
        [functools.partial(local_work, c) for c in range(steps)],
    )

    *attended, sums = pl.pallas_call(
        functools.partial(sums_kernel, steps),
        in_specs=[SMEM, SMEM] + [VMEM] * (3 * steps + 5),
        out_specs=[VMEM] * (steps + 1),
        out_shape=[chunk_wide] * steps + [sums_shape],
        scratch_shapes=[held_bf, token_bf],
        input_output_aliases={3 + steps + c: c for c in range(steps)},
        compiler_params=params(False),
        cost_estimate=estimate(),
        name="token_sums",
    )(*scalars, norm_gain, *near(*query, *attended, *grad), *entering)
    sums = from_all(sums, "head")

    *exits, gain_part = pl.pallas_call(
        functools.partial(exit_kernel, features, steps, len(sums)),
        in_specs=[SMEM, SMEM] + [VMEM] * (3 * steps + 1 + len(sums)),
        out_specs=[VMEM] * 5,
        out_shape=[part_shape] * 4 + [gain_shape],
        scratch_shapes=[token_f, token_f, held_f],
        compiler_params=params(False),
        cost_estimate=estimate(),
        name="start_grads",
    )(*scalars, norm_gain, *sums, *near(*turned, *attended, *grad))
    gain_total = SwapSum(gain_part, "ctx")

    natives, key_local, value_local = [], [None] * steps, [None] * steps
    exit_state = []

    def grad_work(c, after):
        block = pl.BlockSpec((CHUNK, heads, width), lambda i: (c, 0, 0))
        given = [
            *scalars, *near(query[c], key_major, value_major, attended[c], grad[c], entry[c]),
            norm_gain, *entering, *sums, after, gain_total.x, *near(*exit_state),
        ]
        *natives[:], key_local[c], value_local[c], next_state, tick = pl.pallas_call(
            functools.partial(grad_kernel, features, c, steps, len(sums)),
            grid=(1,),
            in_specs=[SMEM, SMEM] + [VMEM] * (11 + len(sums)) + [ANY] * 2 + [VMEM] * len(exit_state) + [HBM] * len(natives),
            out_specs=[block, block, VMEM, VMEM, VMEM, VMEM],
            out_shape=[native_shape, native_shape, chunk_shape, chunk_shape, held_f, tick_shape],
            scratch_shapes=[
                held_f, token_f, token_f, token_bf, token_bf, pltpu.VMEM((2, CHUNK, CHUNK), BF16),
                chunk_shape, chunk_shape,
            ],
            input_output_aliases={len(given) + i: i for i in range(len(natives))},
            compiler_params=params(),
            cost_estimate=estimate(),
            name="chunk_grads",
        )(*given, *natives)
        exit_state[:] = [next_state]
        gain_total.step(tick)
        return tick

    leaving = pair_scan(
        list(exits), True, scalars, rows, hops,
        [functools.partial(grad_work, c) for c in reversed(range(steps))],
    )
    normed, grad_queries = natives
    grad_gain = gain_total.result(leaving[0]) / math.sqrt(rows * shards)

    grad_keys, grad_values = pl.pallas_call(
        functools.partial(last_kernel, steps),
        in_specs=[SMEM, SMEM] + [VMEM] * (2 * steps + 6),
        out_specs=[HBM] * 2,
        out_shape=[native_shape] * 2,
        scratch_shapes=[
            held_bf, token_bf, chunk_shape, chunk_shape,
            pltpu.VMEM((steps, CHUNK, heads, width), BF16),
            pltpu.VMEM((steps, CHUNK, heads, width), BF16),
            pltpu.SemaphoreType.DMA((2, steps)),
        ],
        compiler_params=params(False),
        cost_estimate=estimate(),
        name="key_grads",
    )(*scalars, *near(key_major, value_major, *key_local, *value_local), *leaving)
    return normed, grad_queries, grad_keys, grad_values, grad_gain


def solution(mesh):
    tokens = P("ctx", "head", None)
    in_specs = (tokens, tokens, tokens, tokens, P("head", None), P())
    out_specs = (tokens, tokens, tokens, tokens, P("head", None))
    return jax.shard_map(local, mesh=mesh, in_specs=in_specs, out_specs=out_specs, check_vma=False)
```

```python
import functools
import math

import jax
import jax.numpy as jnp
from jax import lax
from jax.experimental import pallas as pl
from jax.experimental.pallas import tpu as pltpu
from jax.sharding import PartitionSpec as P

CHUNK = 256
LANES = 128
EPSILON = 1e-06
FAR = 2**30
VMEM_LIMIT = 20 * 1024 * 1024
GROUP = 16
UNROLL = 8

F32 = jnp.float32
BF16 = jnp.bfloat16


def dot_nn(a, b):
    return lax.dot_general(a, b, (((1,), (0,)), ((), ())), preferred_element_type=F32)


def dot_nt(a, b):
    return lax.dot_general(a, b, (((1,), (1,)), ((), ())), preferred_element_type=F32)


def dot_tn(a, b):
    return lax.dot_general(a, b, (((0,), (0,)), ((), ())), preferred_element_type=F32)


def block_diagonal(a, b):
    nothing = jnp.zeros_like(a)
    return jnp.concatenate(
        [jnp.concatenate([a, nothing], axis=1), jnp.concatenate([nothing, b], axis=1)], axis=0
    )


def side_by_side(a, b):
    return jnp.concatenate([a, b], axis=1)


def first_start_from(starts, row):
    best = jnp.int32(FAR)
    for i in range(starts.shape[0]):
        best = jnp.minimum(best, jnp.where(starts[i] >= row, starts[i], FAR))
    return best


def last_start_to(starts, row):
    best = jnp.int32(0)
    for i in range(starts.shape[0]):
        best = jnp.maximum(best, jnp.where(starts[i] <= row, starts[i], 0))
    return best


def token_rows(first, shape, axis):
    return first + lax.broadcasted_iota(jnp.int32, shape, axis)


def within_mask(starts, first, axis):
    shape = (CHUNK, CHUNK)
    t = token_rows(first, shape, axis)
    s = token_rows(first, shape, 1 - axis)
    begin = jnp.zeros(shape, jnp.int32)
    for i in range(starts.shape[0]):
        begin = jnp.maximum(begin, jnp.where(starts[i] <= t, starts[i], 0))
    return jnp.where((s <= t) & (s >= begin), 1.0, 0.0).astype(BF16)


def before_mask(first, bound, dtype):
    return jnp.where(token_rows(first, (CHUNK, LANES), 0) < bound, 1.0, 0.0).astype(dtype)


def from_mask(first, bound, dtype):
    return jnp.where(token_rows(first, (CHUNK, LANES), 0) >= bound, 1.0, 0.0).astype(dtype)


def own_head(base, j, heads):
    return lax.rem(j + base[1] * (heads // 2), heads)


def to_major(block, out, first):
    for i in range(0, block.shape[0], GROUP):
        rows = pl.ds(pl.multiple_of(first + i, GROUP), GROUP)
        out[:, rows, :] = jnp.transpose(block[i : i + GROUP], (1, 0, 2))


def to_native(major, block):
    for i in range(0, block.shape[0], GROUP):
        block[i : i + GROUP] = jnp.transpose(major[:, i : i + GROUP, :], (1, 0, 2))


def chunk_rows(step):
    return pl.ds(pl.multiple_of(step * CHUNK, CHUNK), CHUNK)


def state_kernel(starts, base, k_ref, v_ref, o0, o1, o2, o3, k_major, v_major, total):
    heads = k_ref.shape[1]
    step, steps = pl.program_id(0), pl.num_programs(0)
    first = base[0] + step * CHUNK
    bound = last_start_to(starts, base[0] + steps * CHUNK - 1)
    rows = chunk_rows(step)

    @pl.when(step == 0)
    def _():
        total[...] = jnp.zeros_like(total)

    to_major(k_ref, k_major, step * CHUNK)
    to_major(v_ref, v_major, step * CHUNK)

    @pl.when(bound < first + CHUNK)
    def _():
        leave = from_mask(first, bound, BF16)
        for j in range(heads):
            head = own_head(base, j, heads)
            total[j] += dot_tn(k_major[head, rows, :] * leave, v_major[head, rows, :])

    @pl.when(step == steps - 1)
    def _():
        part = heads // 4
        for i, out in enumerate((o0, o1, o2, o3)):
            out[...] = total[i * part : (i + 1) * part]


def local_kernel(
    chunk, starts, base, q_ref, g_ref, k_major, v_major, *refs
):
    q_ref, g_ref = q_ref.at[pl.ds(chunk * CHUNK, CHUNK)], g_ref.at[pl.ds(chunk * CHUNK, CHUNK)]
    state_in = refs[1] if chunk else None
    q_major, g_major, att_ref, entry_ref, q_turned, state_out, tick, mask, enter, leave, reach = refs[2 if chunk else 1 :]
    tick[...] = jnp.zeros_like(tick)
    heads, width = q_ref.shape[1:]
    first = base[0] + chunk * CHUNK
    rows = slice(chunk * CHUNK, (chunk + 1) * CHUNK)
    enter_end = first_start_from(starts, first)
    leave_start = last_start_to(starts, first + CHUNK - 1)
    keep = jnp.where(enter_end >= first + CHUNK, 1.0, 0.0).astype(F32)
    to_major(q_ref, q_major, 0)
    to_major(g_ref, g_major, 0)
    reach[...] = before_mask(first, first_start_from(starts, base[0]), BF16)
    mask[...] = within_mask(starts, first, 0)
    enter[...] = before_mask(first, enter_end, BF16)
    leave[...] = from_mask(first, leave_start, BF16)
    for p in range(0, heads, 2):
        pair = (p, p + 1)
        if chunk:
            entry = [state_in[j].astype(BF16) for j in pair]
            inter = dot_nn(
                side_by_side(*[q_major[j] * enter[...] for j in pair]), block_diagonal(*entry)
            )
        for i, j in enumerate(pair):
            query, key, value = q_major[j], k_major[j, rows, :], v_major[j, rows, :]
            scores = dot_nt(query, key).astype(BF16) * mask[...]
            turned = jnp.transpose(key * leave[...], (1, 0))
            both = dot_nn(jnp.concatenate([scores, turned], axis=0), value)
            att, after = both[:CHUNK], both[CHUNK:]
            q_turned[j] = jnp.transpose(query * reach[...], (1, 0))
            if chunk:
                att += inter[:, i * width : (i + 1) * width]
                after += keep * state_in[j]
                entry_ref[j] = entry[i]
            else:
                entry_ref[j] = jnp.zeros(entry_ref.shape[1:], BF16)
            att_ref[j] = att
            state_out[j] = after


def load_states(parts, held):
    part = parts[0].shape[0]
    for i, ref in enumerate(parts):
        held[i * part : (i + 1) * part] = ref[...].astype(held.dtype)


def eye():
    shape = (LANES, LANES)
    return lax.broadcasted_iota(jnp.int32, shape, 0) == lax.broadcasted_iota(jnp.int32, shape, 1)


def column_of(row):
    return jnp.sum(jnp.where(eye(), row, 0.0), axis=1, keepdims=True)


def row_of(column):
    return jnp.sum(jnp.where(eye(), column, 0.0), axis=0, keepdims=True)


def sums_kernel(steps, starts, base, gain, *refs):
    q_refs, att_refs, g_refs = refs[:steps], refs[steps : 2 * steps], refs[2 * steps : 3 * steps]
    states = refs[3 * steps : 3 * steps + 4]
    att_outs = refs[3 * steps + 4 : 4 * steps + 4]
    sums, held, enter = refs[4 * steps + 4 :]
    heads = q_refs[0].shape[0]
    bound = first_start_from(starts, base[0])
    load_states(states, held)
    blocks = CHUNK // LANES
    for step in range(steps):
        q_ref, att_ref, g_ref, att_out = q_refs[step], att_refs[step], g_refs[step], att_outs[step]
        enter[...] = before_mask(base[0] + step * CHUNK, bound, BF16)
        nothing = jnp.zeros((CHUNK, LANES), F32)

        def body(p, carry, q_ref=q_ref, att_ref=att_ref, g_ref=g_ref, att_out=att_out):
            squares, cross = carry
            places = [2 * p, 2 * p + 1]
            own = [own_head(base, j, heads) for j in places]
            inter = dot_nn(
                side_by_side(*[q_ref[head] * enter[...] for head in own]),
                block_diagonal(*[held[j] for j in places]),
            )
            for i, head in enumerate(own):
                att = att_ref[head] + inter[:, i * LANES : (i + 1) * LANES]
                att_out[head] = att
                weighted = g_ref[head].astype(F32) * gain[pl.ds(head, 1), :]
                squares = squares + att * att
                cross = cross + weighted * att
            return squares, cross

        squares, cross = lax.fori_loop(0, heads // 2, body, (nothing, nothing), unroll=UNROLL // 2)
        for i in range(blocks):
            part = slice(i * LANES, (i + 1) * LANES)
            place = step * blocks + i
            sums[place : place + 1, :] = row_of(jnp.sum(squares[part], axis=1, keepdims=True))
            place += steps * blocks
            sums[place : place + 1, :] = row_of(jnp.sum(cross[part], axis=1, keepdims=True))


def norm_columns(sums, step, steps, features, inverse, factor):
    blocks = CHUNK // LANES

    def total(place):
        return sum(ref[place : place + 1, :] for ref in sums)

    for i in range(blocks):
        rows = slice(i * LANES, (i + 1) * LANES)
        place = step * blocks + i
        square = total(place)
        cross = total(steps * blocks + place)
        inv = 1.0 / jnp.sqrt(square / features + EPSILON)
        fac = inv * inv * inv * cross / features
        inverse[rows, :] = jnp.broadcast_to(column_of(inv), (LANES, LANES))
        factor[rows, :] = jnp.broadcast_to(column_of(fac), (LANES, LANES))


def exit_kernel(features, steps, count, starts, base, gain, *refs):
    sums, refs = refs[:count], refs[count:]
    q_refs, att_refs, g_refs = refs[:steps], refs[steps : 2 * steps], refs[2 * steps : 3 * steps]
    outs = refs[3 * steps : 3 * steps + 4]
    gain_sum, inverse, factor, total = refs[3 * steps + 4 :]
    heads = q_refs[0].shape[0]
    total[...] = jnp.zeros_like(total)
    gain_sum[...] = jnp.zeros_like(gain_sum)
    for step in range(steps):
        norm_columns(sums, step, steps, features, inverse, factor)

        def body(j, carry, step=step):
            head = own_head(base, j, heads)
            upstream = g_refs[step][head].astype(F32)
            att = att_refs[step][head]
            scaled = inverse[...] * upstream
            gain_sum[pl.ds(head, 1), :] += jnp.sum(scaled * att, axis=0, keepdims=True)
            grad = (scaled * gain[pl.ds(head, 1), :] - att * factor[...]).astype(BF16)
            total[j] += dot_nn(q_refs[step][head], grad)
            return carry

        lax.fori_loop(0, heads, body, 0, unroll=UNROLL)

    part = heads // 4
    for i, out in enumerate(outs):
        out[:part] = total[i * part : (i + 1) * part]
    outs[2][part] = jnp.zeros(outs[2].shape[1:], F32)
    outs[2][part, :heads, :] = gain_sum[...]


def grad_kernel(
    features, chunk, steps, count, starts, base, q_ref, k_ref, v_ref, att_ref, g_ref, entry_ref, gain,
    r0, r1, r2, r3, *refs
):
    sums, refs = refs[:count], refs[count:]
    state_in = refs[1] if chunk < steps - 1 else None
    normed, grad_q, grad_k, grad_v, state_out, tick = refs[-14:-8]
    held, inverse, factor, enter, leave, masks, normed_major, grad_major = refs[-8:]
    tick[...] = jnp.zeros_like(tick)
    heads, _, width = q_ref.shape
    first = base[0] + chunk * CHUNK
    rows = slice(chunk * CHUNK, (chunk + 1) * CHUNK)
    bound = first_start_from(starts, base[0])
    reach = jnp.where(bound >= first, 1.0, 0.0).astype(F32)
    enter_end = first_start_from(starts, first)
    leave_start = last_start_to(starts, first + CHUNK - 1)
    keep = jnp.where(enter_end >= first + CHUNK, 1.0, 0.0).astype(F32)
    load_states((r0, r1, r2, r3), held)
    norm_columns(sums, chunk, steps, features, inverse, factor)
    enter[...] = before_mask(first, enter_end, BF16)
    leave[...] = from_mask(first, leave_start, BF16)
    masks[0] = within_mask(starts, first, 0)
    masks[1] = within_mask(starts, first, 1)
    for p in range(0, heads, 2):
        places = (p, p + 1)
        own = [own_head(base, j, heads) for j in places]
        grads, entries = [], []
        for j, head in zip(places, own):
            scale = gain[pl.ds(head, 1), :]
            att = att_ref[head]
            scaled = att * inverse[...]
            normed_major[head] = (scaled * scale).astype(BF16)
            weighted = g_ref[head].astype(F32) * scale
            grads.append((inverse[...] * weighted - att * factor[...]).astype(BF16))
            entries.append((entry_ref[head].astype(F32) + reach * held[j]).astype(BF16))
        inter = dot_nt(
            side_by_side(*[grad * enter[...] for grad in grads]), block_diagonal(*entries)
        )
        if state_in is not None:
            exits = block_diagonal(*[state_in[head].astype(BF16) for head in own])
            key_inter = dot_nt(side_by_side(*[v_ref[head, rows, :] * leave[...] for head in own]), exits)
            value_inter = dot_nn(side_by_side(*[k_ref[head, rows, :] * leave[...] for head in own]), exits)
        for i, (head, grad) in enumerate(zip(own, grads)):
            lanes = slice(i * width, (i + 1) * width)
            query, key, value = q_ref[head], k_ref[head, rows, :], v_ref[head, rows, :]
            scores = dot_nt(grad, value).astype(BF16) * masks[0]
            grad_major[head] = (dot_nn(scores, key) + inter[:, lanes]).astype(BF16)
            key_grad = dot_tn(scores, query)
            scores = dot_nt(key, query).astype(BF16) * masks[1]
            value_grad = dot_nn(scores, grad)
            before = dot_tn(query * enter[...], grad)
            if state_in is not None:
                key_grad += key_inter[:, lanes]
                value_grad += value_inter[:, lanes]
                before += keep * state_in[head]
            grad_k[head] = key_grad.astype(BF16)
            grad_v[head] = value_grad.astype(BF16)
            state_out[head] = before
    to_native(normed_major, normed)
    to_native(grad_major, grad_q)


def last_kernel(steps, starts, base, k_ref, v_ref, *refs):
    gk_refs, gv_refs, states = refs[:steps], refs[steps : 2 * steps], refs[2 * steps : 2 * steps + 4]
    grad_k, grad_v, held, leave, k_rows, v_rows, k_block, v_block, sems = refs[2 * steps + 4 :]
    heads, _, width = k_ref.shape
    load_states(states, held)
    bound = last_start_to(starts, base[0] + steps * CHUNK - 1)
    copies = []
    for step in range(steps):
        rows = slice(step * CHUNK, (step + 1) * CHUNK)
        leave[...] = from_mask(base[0] + step * CHUNK, bound, BF16)

        def body(p, carry, step=step, rows=rows):
            places = (2 * p, 2 * p + 1)
            own = [own_head(base, j, heads) for j in places]
            exits = block_diagonal(*[held[j] for j in places])
            key_inter = dot_nt(side_by_side(*[v_ref[head, rows, :] * leave[...] for head in own]), exits)
            value_inter = dot_nn(side_by_side(*[k_ref[head, rows, :] * leave[...] for head in own]), exits)
            for i, head in enumerate(own):
                lanes = slice(i * width, (i + 1) * width)
                k_rows[head] = (gk_refs[step][head].astype(F32) + key_inter[:, lanes]).astype(BF16)
                v_rows[head] = (gv_refs[step][head].astype(F32) + value_inter[:, lanes]).astype(BF16)
            return carry

        lax.fori_loop(0, heads // 2, body, 0, unroll=UNROLL // 2)
        for i, (major, block, out) in enumerate(((k_rows, k_block, grad_k), (v_rows, v_block, grad_v))):
            to_native(major, block.at[step])
            copy = pltpu.make_async_copy(block.at[step], out.at[rows], sems.at[i, step])
            copy.start()
            copies.append(copy)
    for copy in copies:
        copy.wait()


SMEM = pl.BlockSpec(memory_space=pltpu.SMEM)


VMEM = pl.BlockSpec(memory_space=pltpu.VMEM)
HBM = pl.BlockSpec(memory_space=pltpu.HBM)
ANY = pl.BlockSpec(memory_space=pl.ANY)


def params(grid=True):
    order = ("arbitrary",) if grid else None
    return pltpu.CompilerParams(dimension_semantics=order, vmem_limit_bytes=VMEM_LIMIT)


def estimate():
    return pl.CostEstimate(flops=1, bytes_accessed=1, transcendentals=0)


def far(*arrays):
    return [pltpu.with_memory_space_constraint(x, pltpu.HBM) for x in arrays]


def near(*arrays):
    return [pltpu.with_memory_space_constraint(x, pltpu.VMEM) for x in arrays]


def whole(shape):
    return pl.BlockSpec(shape, lambda c: (0,) * len(shape))


def keep_of(starts, row, rows):
    return jnp.where(first_start_from(starts, row) >= row + rows, 1.0, 0.0).astype(F32)


def pair_keeps(starts, base, rows, backward):
    side = base[1]
    row = base[0] - side * rows
    low, high = keep_of(starts, row, rows), keep_of(starts, row + rows, rows)
    if backward:
        return side == 1, high, low
    return side == 0, low, high


def pair_kernel(rows, backward, starts, base, mine, theirs, tick, first, pair):
    lead, _, second_keep = pair_keeps(starts, base, rows, backward)
    other = theirs[: mine.shape[0]]
    first[...] = jnp.where(lead, mine[...], other)
    pair[...] = jnp.where(lead, other, mine[...]) + second_keep * first[...]


def hop_kernel(rows, backward, starts, base, pair, moved, tick, out):
    _, first_keep, second_keep = pair_keeps(starts, base, rows, backward)
    out[...] = pair[...] + (first_keep * second_keep) * moved[...]


def split_kernel(rows, backward, starts, base, first, moved, tick, own, other):
    lead, first_keep, _ = pair_keeps(starts, base, rows, backward)
    early = moved[...]
    late = first[...] + first_keep * early
    own[...] = jnp.where(lead, early, late)
    other[...] = jnp.where(lead, late, early)


def small_call(kernel, name, count, starts, base, *arrays):
    shape = jax.ShapeDtypeStruct(arrays[0].shape, F32)
    return pl.pallas_call(
        kernel,
        in_specs=[SMEM, SMEM, VMEM, VMEM, ANY],
        out_specs=[VMEM] * count,
        out_shape=[shape] * count,
        compiler_params=pltpu.CompilerParams(vmem_limit_bytes=8 * 1024 * 1024),
        cost_estimate=estimate(),
        name=name,
    )(starts, base, *arrays)


def pair_scan(parts, backward, scalars, rows, hops, works):
    half = len(parts) // 2
    works = list(works)
    shards = lax.axis_size("ctx")
    swap = [(i, i ^ 1) for i in range(shards)]
    if backward:
        step = [(i, i - 2) for i in range(2, shards)]
    else:
        step = [(i, i + 2) for i in range(shards - 2)]

    def work(i, after):
        return works.pop(0)(after) if len(works) > 1 and (i == half - 1 or not firsts) else after

    def call(kernel, name, count, *arrays):
        return small_call(functools.partial(kernel, rows, backward), name, count, *scalars, *arrays)

    arrived = [lax.ppermute(p, "ctx", swap) for p in parts[half:]]
    after = parts[half]
    firsts, pairs, moved = [], [], []
    for i, (mine, theirs) in enumerate(zip(parts[:half], arrived)):
        first, pair = call(pair_kernel, "pair_states", 2, mine, theirs, work(i, after))
        firsts.append(first)
        pairs.append(pair)
        moved.append(lax.ppermute(pair, "ctx", step))
        after = pair
    for _ in range(1, hops):
        for i, pair in enumerate(pairs):
            (after,) = call(hop_kernel, "chain_states", 1, pair, moved[i], work(i, after))
            moved[i] = lax.ppermute(after, "ctx", step)
    own_out, got = [], []
    for i, (first, incoming) in enumerate(zip(firsts, moved)):
        own, after = call(split_kernel, "split_states", 2, first, incoming, work(i, after))
        own_out.append(own)
        got.append(lax.ppermute(after, "ctx", swap))
    while works:
        works.pop(0)(after)
    return own_out + got, arrived[0]


def pair_gain_kernel(own, theirs, out):
    out[...] = own[...] + theirs[theirs.shape[0] - 1, : own.shape[0], :]


def sum_kernel(*refs):
    out = refs[-1]
    out[...] = sum(ref[...] for ref in refs[:-2])


def sum_gains(parts, tick):
    return pl.pallas_call(
        sum_kernel,
        in_specs=[VMEM] * len(parts) + [ANY],
        out_specs=VMEM,
        out_shape=jax.ShapeDtypeStruct(parts[0].shape, F32),
        compiler_params=pltpu.CompilerParams(vmem_limit_bytes=8 * 1024 * 1024),
        cost_estimate=estimate(),
        name="gain_sum",
    )(*parts, tick)


def pair_gain(own, theirs):
    return pl.pallas_call(
        pair_gain_kernel,
        in_specs=[VMEM, VMEM],
        out_specs=VMEM,
        out_shape=jax.ShapeDtypeStruct(own.shape, F32),
        compiler_params=pltpu.CompilerParams(vmem_limit_bytes=8 * 1024 * 1024),
        cost_estimate=estimate(),
        name="pair_gain",
    )(own, theirs)


def from_all(x, axis):
    size = lax.axis_size(axis)
    return [x] + [
        lax.ppermute(x, axis, [(i, (i + d) % size) for i in range(size)]) for d in range(1, size)
    ]


def branch_kernel(span, total, counts, starts, out):
    docs = starts.shape[0]
    crossed = jnp.int32(0)
    for i in range(docs):
        end = starts[i + 1] if i + 1 < docs else total
        crossed = jnp.maximum(crossed, lax.div(end - 1, span) - lax.div(starts[i], span))
    out[0] = sum((crossed > count).astype(jnp.int32) for count in counts[:-1])


def local(*args):
    rows, document_starts = args[0].shape[0], args[-1]
    shards = lax.axis_size("ctx")
    most = shards // 2 - 1
    counts = sorted({min(1, most), min(2, most), most})
    index = pl.pallas_call(
        functools.partial(branch_kernel, 2 * rows, shards * rows, counts),
        in_specs=[SMEM],
        out_specs=SMEM,
        out_shape=jax.ShapeDtypeStruct((1,), jnp.int32),
        name="branch",
    )(document_starts)
    return lax.switch(index[0], [functools.partial(with_hops, count) for count in counts], *args)


def with_hops(hops, queries, key_rows, value_rows, grad_normed, norm_gain, document_starts):
    rows, heads, width = queries.shape
    shards = lax.axis_size("ctx")
    shard = lax.axis_index("ctx")
    features = heads * lax.axis_size("head") * width
    steps = rows // CHUNK
    part = heads // 4
    base = jnp.stack([shard * rows, lax.rem(shard, 2)]).astype(jnp.int32)

    native = pl.BlockSpec((CHUNK, heads, width), lambda c: (c, 0, 0))
    native_shape = jax.ShapeDtypeStruct((rows, heads, width), BF16)
    major_shape = pltpu.VMEM((heads, rows, width), BF16)
    chunk_shape = pltpu.VMEM((heads, CHUNK, width), BF16)
    turned_shape = pltpu.VMEM((heads, width, CHUNK), BF16)
    chunk_wide = pltpu.VMEM((heads, CHUNK, width), F32)
    part_spec = pl.BlockSpec((part, width, width), lambda c: (0, 0, 0))
    part_shape = jax.ShapeDtypeStruct((part, width, width), F32)
    held_bf = pltpu.VMEM((heads, width, width), BF16)
    held_f = pltpu.VMEM((heads, width, width), F32)
    token_bf = pltpu.VMEM((CHUNK, width), BF16)
    token_f = pltpu.VMEM((CHUNK, width), F32)
    mask_bf = pltpu.VMEM((CHUNK, CHUNK), BF16)
    sum_rows = 2 * rows // LANES
    sums_shape = jax.ShapeDtypeStruct((sum_rows, LANES), F32)
    gain_shape = jax.ShapeDtypeStruct((heads, width), F32)
    tick_shape = jax.ShapeDtypeStruct((8, LANES), F32)
    scalars = (document_starts, base)

    *states, key_major, value_major = pl.pallas_call(
        state_kernel,
        grid=(steps,),
        in_specs=[SMEM, SMEM, native, native],
        out_specs=[part_spec] * 4 + [VMEM] * 2,
        out_shape=[part_shape] * 4 + [major_shape] * 2,
        scratch_shapes=[held_f],
        compiler_params=params(),
        cost_estimate=estimate(),
        name="end_states",
    )(*scalars, *far(key_rows, value_rows))

    query, grad, attended, entry, turned = [], [], [], [], []
    state = []

    def local_work(c, after):
        *made, next_state, tick = pl.pallas_call(
            functools.partial(local_kernel, c),
            in_specs=[SMEM, SMEM] + [VMEM] * 4 + [ANY] + [VMEM] * min(c, 1),
            out_specs=[VMEM] * 7,
            out_shape=[chunk_shape, chunk_shape, chunk_wide, held_bf, turned_shape, held_f, tick_shape],
            scratch_shapes=[mask_bf, token_bf, token_bf, token_bf],
            compiler_params=params(False),
            cost_estimate=estimate(),
            name="local_attention",
        )(*scalars, *near(queries, grad_normed, key_major, value_major), after, *near(*state))
        for kept, one in zip((query, grad, attended, entry, turned), made):
            kept.append(one)
        state[:] = [next_state]
        return tick

    entering, _ = pair_scan(
        list(states), False, scalars, rows, hops,
        [functools.partial(local_work, c) for c in range(steps)],
    )

    *attended, sums = pl.pallas_call(
        functools.partial(sums_kernel, steps),
        in_specs=[SMEM, SMEM] + [VMEM] * (3 * steps + 5),
        out_specs=[VMEM] * (steps + 1),
        out_shape=[chunk_wide] * steps + [sums_shape],
        scratch_shapes=[held_bf, token_bf],
        input_output_aliases={3 + steps + c: c for c in range(steps)},
        compiler_params=params(False),
        cost_estimate=estimate(),
        name="token_sums",
    )(*scalars, norm_gain, *near(*query, *attended, *grad), *entering)
    sums = from_all(sums, "head")

    *exits, gain_part = pl.pallas_call(
        functools.partial(exit_kernel, features, steps, len(sums)),
        in_specs=[SMEM, SMEM] + [VMEM] * (3 * steps + 1 + len(sums)),
        out_specs=[VMEM] * 5,
        out_shape=[part_shape] * 2
        + [jax.ShapeDtypeStruct((part + 1, width, width), F32), part_shape, gain_shape],
        scratch_shapes=[token_f, token_f, held_f],
        compiler_params=params(False),
        cost_estimate=estimate(),
        name="start_grads",
    )(*scalars, norm_gain, *sums, *near(*turned, *attended, *grad))

    natives, key_local, value_local = [], [None] * steps, [None] * steps
    exit_state = []

    def grad_work(c, after):
        block = pl.BlockSpec((CHUNK, heads, width), lambda i: (c, 0, 0))
        given = [
            *scalars, *near(query[c], key_major, value_major, attended[c], grad[c], entry[c]),
            norm_gain, *entering, *sums, after, *near(*exit_state),
        ]
        *natives[:], key_local[c], value_local[c], next_state, tick = pl.pallas_call(
            functools.partial(grad_kernel, features, c, steps, len(sums)),
            grid=(1,),
            in_specs=[SMEM, SMEM] + [VMEM] * (11 + len(sums)) + [ANY] + [VMEM] * len(exit_state) + [HBM] * len(natives),
            out_specs=[block, block, VMEM, VMEM, VMEM, VMEM],
            out_shape=[native_shape, native_shape, chunk_shape, chunk_shape, held_f, tick_shape],
            scratch_shapes=[
                held_f, token_f, token_f, token_bf, token_bf, pltpu.VMEM((2, CHUNK, CHUNK), BF16),
                chunk_shape, chunk_shape,
            ],
            input_output_aliases={len(given) + i: i for i in range(len(natives))},
            compiler_params=params(),
            cost_estimate=estimate(),
            name="chunk_grads",
        )(*given, *natives)
        exit_state[:] = [next_state]
        return tick

    leaving, arrived = pair_scan(
        list(exits), True, scalars, rows, hops,
        [functools.partial(grad_work, c) for c in reversed(range(steps))],
    )
    normed, grad_queries = natives
    gains = [pair_gain(gain_part, arrived)]
    for distance in range(2, shards, 2):
        gains.append(lax.ppermute(gains[0], "ctx", [(i, i ^ distance) for i in range(shards)]))
    grad_gain = sum_gains(gains, key_local[0]) / math.sqrt(rows * shards)

    grad_keys, grad_values = pl.pallas_call(
        functools.partial(last_kernel, steps),
        in_specs=[SMEM, SMEM] + [VMEM] * (2 * steps + 6),
        out_specs=[HBM] * 2,
        out_shape=[native_shape] * 2,
        scratch_shapes=[
            held_bf, token_bf, chunk_shape, chunk_shape,
            pltpu.VMEM((steps, CHUNK, heads, width), BF16),
            pltpu.VMEM((steps, CHUNK, heads, width), BF16),
            pltpu.SemaphoreType.DMA((2, steps)),
        ],
        compiler_params=params(False),
        cost_estimate=estimate(),
        name="key_grads",
    )(*scalars, *near(key_major, value_major, *key_local, *value_local), *leaving)
    return normed, grad_queries, grad_keys, grad_values, grad_gain


def solution(mesh):
    tokens = P("ctx", "head", None)
    in_specs = (tokens, tokens, tokens, tokens, P("head", None), P())
    out_specs = (tokens, tokens, tokens, tokens, P("head", None))
    return jax.shard_map(local, mesh=mesh, in_specs=in_specs, out_specs=out_specs, check_vma=False)
```

```python
import functools
import math

import jax
import jax.numpy as jnp
from jax import lax
from jax.experimental import pallas as pl
from jax.experimental.pallas import tpu as pltpu
from jax.sharding import PartitionSpec as P

CHUNK = 256
LANES = 128
EPSILON = 1e-06
FAR = 2**30
VMEM_LIMIT = 14 * 1024 * 1024
GROUP = 16
UNROLL = 8

F32 = jnp.float32
BF16 = jnp.bfloat16


def dot_nn(a, b):
    return lax.dot_general(a, b, (((1,), (0,)), ((), ())), preferred_element_type=F32)


def dot_nt(a, b):
    return lax.dot_general(a, b, (((1,), (1,)), ((), ())), preferred_element_type=F32)


def dot_tn(a, b):
    return lax.dot_general(a, b, (((0,), (0,)), ((), ())), preferred_element_type=F32)


def block_diagonal(a, b):
    nothing = jnp.zeros_like(a)
    return jnp.concatenate(
        [jnp.concatenate([a, nothing], axis=1), jnp.concatenate([nothing, b], axis=1)], axis=0
    )


def side_by_side(a, b):
    return jnp.concatenate([a, b], axis=1)


def first_start_from(starts, row):
    best = jnp.int32(FAR)
    for i in range(starts.shape[0]):
        best = jnp.minimum(best, jnp.where(starts[i] >= row, starts[i], FAR))
    return best


def last_start_to(starts, row):
    best = jnp.int32(0)
    for i in range(starts.shape[0]):
        best = jnp.maximum(best, jnp.where(starts[i] <= row, starts[i], 0))
    return best


def token_rows(first, shape, axis):
    return first + lax.broadcasted_iota(jnp.int32, shape, axis)


def within_mask(starts, first, axis):
    shape = (CHUNK, CHUNK)
    t = token_rows(first, shape, axis)
    s = token_rows(first, shape, 1 - axis)
    begin = jnp.zeros(shape, jnp.int32)
    for i in range(starts.shape[0]):
        begin = jnp.maximum(begin, jnp.where(starts[i] <= t, starts[i], 0))
    return jnp.where((s <= t) & (s >= begin), 1.0, 0.0).astype(BF16)


def before_mask(first, bound, dtype):
    return jnp.where(token_rows(first, (CHUNK, LANES), 0) < bound, 1.0, 0.0).astype(dtype)


def from_mask(first, bound, dtype):
    return jnp.where(token_rows(first, (CHUNK, LANES), 0) >= bound, 1.0, 0.0).astype(dtype)


def own_head(base, j, heads):
    return lax.rem(j + base[1] * (heads // 2), heads)


def to_major(block, out, first):
    for i in range(0, block.shape[0], GROUP):
        rows = pl.ds(pl.multiple_of(first + i, GROUP), GROUP)
        out[:, rows, :] = jnp.transpose(block[i : i + GROUP], (1, 0, 2))


def to_native(major, block):
    for i in range(0, block.shape[0], GROUP):
        block[i : i + GROUP] = jnp.transpose(major[:, i : i + GROUP, :], (1, 0, 2))


def chunk_rows(step):
    return pl.ds(pl.multiple_of(step * CHUNK, CHUNK), CHUNK)


def state_kernel(starts, base, k_ref, v_ref, o0, o1, o2, o3, k_major, v_major, total):
    heads = k_ref.shape[1]
    step, steps = pl.program_id(0), pl.num_programs(0)
    first = base[0] + step * CHUNK
    bound = last_start_to(starts, base[0] + steps * CHUNK - 1)
    rows = chunk_rows(step)

    @pl.when(step == 0)
    def _():
        total[...] = jnp.zeros_like(total)

    to_major(k_ref, k_major, step * CHUNK)
    to_major(v_ref, v_major, step * CHUNK)

    @pl.when(bound < first + CHUNK)
    def _():
        leave = from_mask(first, bound, BF16)
        for j in range(heads):
            head = own_head(base, j, heads)
            total[j] += dot_tn(k_major[head, rows, :] * leave, v_major[head, rows, :])

    @pl.when(step == steps - 1)
    def _():
        part = heads // 4
        for i, out in enumerate((o0, o1, o2, o3)):
            out[...] = total[i * part : (i + 1) * part]


def local_kernel(
    chunk, starts, base, q_ref, g_ref, k_major, v_major, *refs
):
    q_ref, g_ref = q_ref.at[pl.ds(chunk * CHUNK, CHUNK)], g_ref.at[pl.ds(chunk * CHUNK, CHUNK)]
    state_in = refs[1] if chunk else None
    q_major, g_major, att_ref, entry_ref, q_turned, state_out, tick, mask, enter, leave, reach = refs[2 if chunk else 1 :]
    tick[...] = jnp.zeros_like(tick)
    heads, width = q_ref.shape[1:]
    first = base[0] + chunk * CHUNK
    rows = slice(chunk * CHUNK, (chunk + 1) * CHUNK)
    enter_end = first_start_from(starts, first)
    leave_start = last_start_to(starts, first + CHUNK - 1)
    keep = jnp.where(enter_end >= first + CHUNK, 1.0, 0.0).astype(F32)
    to_major(q_ref, q_major, 0)
    to_major(g_ref, g_major, 0)
    reach[...] = before_mask(first, first_start_from(starts, base[0]), BF16)
    mask[...] = within_mask(starts, first, 0)
    enter[...] = before_mask(first, enter_end, BF16)
    leave[...] = from_mask(first, leave_start, BF16)
    for p in range(0, heads, 2):
        pair = (p, p + 1)
        if chunk:
            entry = [state_in[j].astype(BF16) for j in pair]
            inter = dot_nn(
                side_by_side(*[q_major[j] * enter[...] for j in pair]), block_diagonal(*entry)
            )
        for i, j in enumerate(pair):
            query, key, value = q_major[j], k_major[j, rows, :], v_major[j, rows, :]
            scores = dot_nt(query, key).astype(BF16) * mask[...]
            turned = jnp.transpose(key * leave[...], (1, 0))
            both = dot_nn(jnp.concatenate([scores, turned], axis=0), value)
            att, after = both[:CHUNK], both[CHUNK:]
            q_turned[j] = jnp.transpose(query * reach[...], (1, 0))
            if chunk:
                att += inter[:, i * width : (i + 1) * width]
                after += keep * state_in[j]
                entry_ref[j] = entry[i]
            else:
                entry_ref[j] = jnp.zeros(entry_ref.shape[1:], BF16)
            att_ref[j] = att.astype(BF16)
            state_out[j] = after


def load_states(parts, held):
    part = parts[0].shape[0]
    for i, ref in enumerate(parts):
        held[i * part : (i + 1) * part] = ref[...].astype(held.dtype)


def eye():
    shape = (LANES, LANES)
    return lax.broadcasted_iota(jnp.int32, shape, 0) == lax.broadcasted_iota(jnp.int32, shape, 1)


def column_of(row):
    return jnp.sum(jnp.where(eye(), row, 0.0), axis=1, keepdims=True)


def row_of(column):
    return jnp.sum(jnp.where(eye(), column, 0.0), axis=0, keepdims=True)


def sums_kernel(steps, starts, base, gain, *refs):
    q_refs, att_refs, g_refs = refs[:steps], refs[steps : 2 * steps], refs[2 * steps : 3 * steps]
    states = refs[3 * steps : 3 * steps + 4]
    att_outs = refs[3 * steps + 4 : 4 * steps + 4]
    sums, held, enter = refs[4 * steps + 4 :]
    heads = q_refs[0].shape[0]
    bound = first_start_from(starts, base[0])
    load_states(states, held)
    blocks = CHUNK // LANES
    for step in range(steps):
        q_ref, att_ref, g_ref, att_out = q_refs[step], att_refs[step], g_refs[step], att_outs[step]
        enter[...] = before_mask(base[0] + step * CHUNK, bound, BF16)
        nothing = jnp.zeros((CHUNK, LANES), F32)

        def body(p, carry, q_ref=q_ref, att_ref=att_ref, g_ref=g_ref, att_out=att_out):
            squares, cross = carry
            places = [2 * p, 2 * p + 1]
            own = [own_head(base, j, heads) for j in places]
            inter = dot_nn(
                side_by_side(*[q_ref[head] * enter[...] for head in own]),
                block_diagonal(*[held[j] for j in places]),
            )
            for i, head in enumerate(own):
                att = att_ref[head].astype(F32) + inter[:, i * LANES : (i + 1) * LANES]
                att_out[head] = att.astype(BF16)
                weighted = g_ref[head].astype(F32) * gain[pl.ds(head, 1), :]
                squares = squares + att * att
                cross = cross + weighted * att
            return squares, cross

        squares, cross = lax.fori_loop(0, heads // 2, body, (nothing, nothing), unroll=UNROLL // 2)
        for i in range(blocks):
            part = slice(i * LANES, (i + 1) * LANES)
            place = step * blocks + i
            sums[place : place + 1, :] = row_of(jnp.sum(squares[part], axis=1, keepdims=True))
            place += steps * blocks
            sums[place : place + 1, :] = row_of(jnp.sum(cross[part], axis=1, keepdims=True))


def norm_columns(sums, step, steps, features, inverse, factor):
    blocks = CHUNK // LANES

    def total(place):
        return sum(ref[place : place + 1, :] for ref in sums)

    for i in range(blocks):
        rows = slice(i * LANES, (i + 1) * LANES)
        place = step * blocks + i
        square = total(place)
        cross = total(steps * blocks + place)
        inv = 1.0 / jnp.sqrt(square / features + EPSILON)
        fac = inv * inv * inv * cross / features
        inverse[rows, :] = jnp.broadcast_to(column_of(inv), (LANES, LANES))
        factor[rows, :] = jnp.broadcast_to(column_of(fac), (LANES, LANES))


def exit_kernel(features, steps, count, parts, starts, base, gain, *refs):
    sums, refs = refs[:count], refs[count:]
    q_refs, att_refs, g_refs = refs[:steps], refs[steps : 2 * steps], refs[2 * steps : 3 * steps]
    outs = refs[3 * steps : 3 * steps + parts]
    gain_sum, inverse, factor, total = refs[3 * steps + parts :]
    heads = q_refs[0].shape[0]
    total[...] = jnp.zeros_like(total)
    gain_sum[...] = jnp.zeros_like(gain_sum)
    for step in range(steps):
        norm_columns(sums, step, steps, features, inverse, factor)

        def body(j, carry, step=step):
            head = own_head(base, j, heads)
            upstream = g_refs[step][head].astype(F32)
            att = att_refs[step][head].astype(F32)
            scaled = inverse[...] * upstream
            gain_sum[pl.ds(head, 1), :] += jnp.sum(scaled * att, axis=0, keepdims=True)
            grad = (scaled * gain[pl.ds(head, 1), :] - att * factor[...]).astype(BF16)
            total[j] += dot_nn(q_refs[step][head], grad)
            return carry

        lax.fori_loop(0, heads, body, 0, unroll=UNROLL)

    part = heads // parts
    for i, out in enumerate(outs):
        out[:part] = total[i * part : (i + 1) * part]
    outs[parts // 2][part] = jnp.zeros(outs[parts // 2].shape[1:], F32)
    outs[parts // 2][part, :heads, :] = gain_sum[...]


def grad_kernel(
    features, chunk, steps, count, starts, base, q_ref, k_ref, v_ref, att_ref, g_ref, entry_ref, gain,
    r0, r1, r2, r3, *refs
):
    sums, refs = refs[:count], refs[count:]
    state_in = refs[1] if chunk < steps - 1 else None
    normed, grad_q, grad_k, grad_v, state_out, tick = refs[-14:-8]
    held, inverse, factor, enter, leave, masks, normed_major, grad_major = refs[-8:]
    tick[...] = jnp.zeros_like(tick)
    heads, _, width = q_ref.shape
    first = base[0] + chunk * CHUNK
    rows = slice(chunk * CHUNK, (chunk + 1) * CHUNK)
    bound = first_start_from(starts, base[0])
    reach = jnp.where(bound >= first, 1.0, 0.0).astype(F32)
    enter_end = first_start_from(starts, first)
    leave_start = last_start_to(starts, first + CHUNK - 1)
    keep = jnp.where(enter_end >= first + CHUNK, 1.0, 0.0).astype(F32)
    load_states((r0, r1, r2, r3), held)
    norm_columns(sums, chunk, steps, features, inverse, factor)
    enter[...] = before_mask(first, enter_end, BF16)
    leave[...] = from_mask(first, leave_start, BF16)
    masks[0] = within_mask(starts, first, 0)
    masks[1] = within_mask(starts, first, 1)
    for p in range(0, heads, 2):
        places = (p, p + 1)
        own = [own_head(base, j, heads) for j in places]
        grads, entries = [], []
        for j, head in zip(places, own):
            scale = gain[pl.ds(head, 1), :]
            att = att_ref[head].astype(F32)
            scaled = att * inverse[...]
            normed_major[head] = (scaled * scale).astype(BF16)
            weighted = g_ref[head].astype(F32) * scale
            grads.append((inverse[...] * weighted - att * factor[...]).astype(BF16))
            entries.append((entry_ref[head].astype(F32) + reach * held[j]).astype(BF16))
        inter = dot_nt(
            side_by_side(*[grad * enter[...] for grad in grads]), block_diagonal(*entries)
        )
        if state_in is not None:
            exits = block_diagonal(*[state_in[head].astype(BF16) for head in own])
            key_inter = dot_nt(side_by_side(*[v_ref[head, rows, :] * leave[...] for head in own]), exits)
            value_inter = dot_nn(side_by_side(*[k_ref[head, rows, :] * leave[...] for head in own]), exits)
        for i, (head, grad) in enumerate(zip(own, grads)):
            lanes = slice(i * width, (i + 1) * width)
            query, key, value = q_ref[head], k_ref[head, rows, :], v_ref[head, rows, :]
            scores = dot_nt(grad, value).astype(BF16) * masks[0]
            grad_major[head] = (dot_nn(scores, key) + inter[:, lanes]).astype(BF16)
            key_grad = dot_tn(scores, query)
            scores = dot_nt(key, query).astype(BF16) * masks[1]
            value_grad = dot_nn(scores, grad)
            before = dot_tn(query * enter[...], grad)
            if state_in is not None:
                key_grad += key_inter[:, lanes]
                value_grad += value_inter[:, lanes]
                before += keep * state_in[head]
            grad_k[head] = key_grad.astype(BF16)
            grad_v[head] = value_grad.astype(BF16)
            state_out[head] = before
    to_native(normed_major, normed)
    to_native(grad_major, grad_q)


def last_kernel(steps, parts, starts, base, k_ref, v_ref, *refs):
    gk_refs, gv_refs, states = refs[:steps], refs[steps : 2 * steps], refs[2 * steps : 2 * steps + parts]
    grad_k, grad_v, held, leave, k_rows, v_rows, k_block, v_block, sems = refs[2 * steps + parts :]
    heads, _, width = k_ref.shape
    load_states(states, held)
    bound = last_start_to(starts, base[0] + steps * CHUNK - 1)
    copies = []
    for step in range(steps):
        rows = slice(step * CHUNK, (step + 1) * CHUNK)
        leave[...] = from_mask(base[0] + step * CHUNK, bound, BF16)

        def body(p, carry, step=step, rows=rows):
            places = (2 * p, 2 * p + 1)
            own = [own_head(base, j, heads) for j in places]
            exits = block_diagonal(*[held[j] for j in places])
            key_inter = dot_nt(side_by_side(*[v_ref[head, rows, :] * leave[...] for head in own]), exits)
            value_inter = dot_nn(side_by_side(*[k_ref[head, rows, :] * leave[...] for head in own]), exits)
            for i, head in enumerate(own):
                lanes = slice(i * width, (i + 1) * width)
                k_rows[head] = (gk_refs[step][head].astype(F32) + key_inter[:, lanes]).astype(BF16)
                v_rows[head] = (gv_refs[step][head].astype(F32) + value_inter[:, lanes]).astype(BF16)
            return carry

        lax.fori_loop(0, heads // 2, body, 0, unroll=UNROLL // 2)
        for i, (major, block, out) in enumerate(((k_rows, k_block, grad_k), (v_rows, v_block, grad_v))):
            to_native(major, block.at[step])
            copy = pltpu.make_async_copy(block.at[step], out.at[rows], sems.at[i, step])
            copy.start()
            copies.append(copy)
    for copy in copies:
        copy.wait()


SMEM = pl.BlockSpec(memory_space=pltpu.SMEM)


VMEM = pl.BlockSpec(memory_space=pltpu.VMEM)
HBM = pl.BlockSpec(memory_space=pltpu.HBM)
ANY = pl.BlockSpec(memory_space=pl.ANY)


def params(grid=True):
    order = ("arbitrary",) if grid else None
    return pltpu.CompilerParams(dimension_semantics=order, vmem_limit_bytes=VMEM_LIMIT)


def estimate():
    return pl.CostEstimate(flops=1, bytes_accessed=1, transcendentals=0)


def far(*arrays):
    return [pltpu.with_memory_space_constraint(x, pltpu.HBM) for x in arrays]


def near(*arrays):
    return [pltpu.with_memory_space_constraint(x, pltpu.VMEM) for x in arrays]


def whole(shape):
    return pl.BlockSpec(shape, lambda c: (0,) * len(shape))


def keep_of(starts, row, rows):
    return jnp.where(first_start_from(starts, row) >= row + rows, 1.0, 0.0).astype(F32)


def pair_keeps(starts, base, rows, backward):
    side = base[1]
    row = base[0] - side * rows
    low, high = keep_of(starts, row, rows), keep_of(starts, row + rows, rows)
    if backward:
        return side == 1, high, low
    return side == 0, low, high


def pair_kernel(rows, backward, starts, base, mine, theirs, tick, first, pair):
    lead, _, second_keep = pair_keeps(starts, base, rows, backward)
    other = theirs[: mine.shape[0]]
    first[...] = jnp.where(lead, mine[...], other)
    pair[...] = jnp.where(lead, other, mine[...]) + second_keep * first[...]


def hop_kernel(rows, backward, starts, base, pair, moved, tick, out):
    _, first_keep, second_keep = pair_keeps(starts, base, rows, backward)
    out[...] = pair[...] + (first_keep * second_keep) * moved[...]


def split_kernel(rows, backward, starts, base, first, moved, tick, own, other):
    lead, first_keep, _ = pair_keeps(starts, base, rows, backward)
    early = moved[...]
    late = first[...] + first_keep * early
    own[...] = jnp.where(lead, early, late)
    other[...] = jnp.where(lead, late, early)


def small_call(kernel, name, count, starts, base, *arrays):
    shape = jax.ShapeDtypeStruct(arrays[0].shape, F32)
    return pl.pallas_call(
        kernel,
        in_specs=[SMEM, SMEM, VMEM, VMEM, ANY],
        out_specs=[VMEM] * count,
        out_shape=[shape] * count,
        compiler_params=pltpu.CompilerParams(vmem_limit_bytes=8 * 1024 * 1024),
        cost_estimate=estimate(),
        name=name,
    )(starts, base, *arrays)


def pair_scan(parts, backward, scalars, rows, hops, works, spare):
    half = len(parts) // 2
    works = list(works)
    shards = lax.axis_size("ctx")
    swap = [(i, i ^ 1) for i in range(shards)]
    if backward:
        step = [(i, i - 2) for i in range(2, shards)]
    else:
        step = [(i, i + 2) for i in range(shards - 2)]

    def work(i, after):
        for _ in range(2 if half == 1 and not firsts else 1):
            if len(works) > spare and (i == half - 1 or not firsts):
                after = works.pop(0)(after)
        return after

    def call(kernel, name, count, *arrays):
        return small_call(functools.partial(kernel, rows, backward), name, count, *scalars, *arrays)

    arrived = [lax.ppermute(p, "ctx", swap) for p in parts[half:]]
    after = parts[half]
    firsts, pairs, moved = [], [], []
    for i, (mine, theirs) in enumerate(zip(parts[:half], arrived)):
        first, pair = call(pair_kernel, "pair_states", 2, mine, theirs, work(i, after))
        firsts.append(first)
        pairs.append(pair)
        moved.append(lax.ppermute(pair, "ctx", step))
        after = pair
    for _ in range(1, hops):
        for i, pair in enumerate(pairs):
            (after,) = call(hop_kernel, "chain_states", 1, pair, moved[i], work(i, after))
            moved[i] = lax.ppermute(after, "ctx", step)
    own_out, got = [], []
    for i, (first, incoming) in enumerate(zip(firsts, moved)):
        own, after = call(split_kernel, "split_states", 2, first, incoming, work(i, after))
        own_out.append(own)
        got.append(lax.ppermute(after, "ctx", swap))
    while works:
        works.pop(0)(after)
    return own_out + got, arrived[0]


def pair_gain_kernel(own, theirs, out):
    out[...] = own[...] + theirs[theirs.shape[0] - 1, : own.shape[0], :]


def sum_kernel(*refs):
    out = refs[-1]
    out[...] = sum(ref[...] for ref in refs[:-2])


def sum_gains(parts, tick):
    return pl.pallas_call(
        sum_kernel,
        in_specs=[VMEM] * len(parts) + [ANY],
        out_specs=VMEM,
        out_shape=jax.ShapeDtypeStruct(parts[0].shape, F32),
        compiler_params=pltpu.CompilerParams(vmem_limit_bytes=8 * 1024 * 1024),
        cost_estimate=estimate(),
        name="gain_sum",
    )(*parts, tick)


def pair_gain(own, theirs):
    return pl.pallas_call(
        pair_gain_kernel,
        in_specs=[VMEM, VMEM],
        out_specs=VMEM,
        out_shape=jax.ShapeDtypeStruct(own.shape, F32),
        compiler_params=pltpu.CompilerParams(vmem_limit_bytes=8 * 1024 * 1024),
        cost_estimate=estimate(),
        name="pair_gain",
    )(own, theirs)


def from_all(x, axis):
    size = lax.axis_size(axis)
    return [x] + [
        lax.ppermute(x, axis, [(i, (i + d) % size) for i in range(size)]) for d in range(1, size)
    ]


def branch_kernel(span, total, counts, starts, out):
    docs = starts.shape[0]
    crossed = jnp.int32(0)
    for i in range(docs):
        end = starts[i + 1] if i + 1 < docs else total
        crossed = jnp.maximum(crossed, lax.div(end - 1, span) - lax.div(starts[i], span))
    out[0] = sum((crossed > count).astype(jnp.int32) for count in counts[:-1])


def local(*args):
    rows, document_starts = args[0].shape[0], args[-1]
    shards = lax.axis_size("ctx")
    most = shards // 2 - 1
    counts = sorted({min(1, most), min(2, most), most})
    index = pl.pallas_call(
        functools.partial(branch_kernel, 2 * rows, shards * rows, counts),
        in_specs=[SMEM],
        out_specs=SMEM,
        out_shape=jax.ShapeDtypeStruct((1,), jnp.int32),
        name="branch",
    )(document_starts)
    return lax.switch(index[0], [functools.partial(with_hops, count) for count in counts], *args)


def with_hops(hops, queries, key_rows, value_rows, grad_normed, norm_gain, document_starts):
    rows, heads, width = queries.shape
    shards = lax.axis_size("ctx")
    shard = lax.axis_index("ctx")
    features = heads * lax.axis_size("head") * width
    steps = rows // CHUNK
    part = heads // 4
    base = jnp.stack([shard * rows, lax.rem(shard, 2)]).astype(jnp.int32)

    native = pl.BlockSpec((CHUNK, heads, width), lambda c: (c, 0, 0))
    native_shape = jax.ShapeDtypeStruct((rows, heads, width), BF16)
    major_shape = pltpu.VMEM((heads, rows, width), BF16)
    chunk_shape = pltpu.VMEM((heads, CHUNK, width), BF16)
    turned_shape = pltpu.VMEM((heads, width, CHUNK), BF16)
    part_spec = pl.BlockSpec((part, width, width), lambda c: (0, 0, 0))
    part_shape = jax.ShapeDtypeStruct((part, width, width), F32)
    held_bf = pltpu.VMEM((heads, width, width), BF16)
    held_f = pltpu.VMEM((heads, width, width), F32)
    token_bf = pltpu.VMEM((CHUNK, width), BF16)
    token_f = pltpu.VMEM((CHUNK, width), F32)
    mask_bf = pltpu.VMEM((CHUNK, CHUNK), BF16)
    sum_rows = 2 * rows // LANES
    sums_shape = jax.ShapeDtypeStruct((sum_rows, LANES), F32)
    gain_shape = jax.ShapeDtypeStruct((heads, width), F32)
    tick_shape = jax.ShapeDtypeStruct((8, LANES), F32)
    scalars = (document_starts, base)

    *states, key_major, value_major = pl.pallas_call(
        state_kernel,
        grid=(steps,),
        in_specs=[SMEM, SMEM, native, native],
        out_specs=[part_spec] * 4 + [VMEM] * 2,
        out_shape=[part_shape] * 4 + [major_shape] * 2,
        scratch_shapes=[held_f],
        compiler_params=params(),
        cost_estimate=estimate(),
        name="end_states",
    )(*scalars, *far(key_rows, value_rows))

    query, grad, attended, entry, turned = [], [], [], [], []
    state = []

    def local_work(c, after):
        *made, next_state, tick = pl.pallas_call(
            functools.partial(local_kernel, c),
            in_specs=[SMEM, SMEM] + [VMEM] * 4 + [ANY] + [VMEM] * min(c, 1),
            out_specs=[VMEM] * 7,
            out_shape=[chunk_shape, chunk_shape, chunk_shape, held_bf, turned_shape, held_f, tick_shape],
            scratch_shapes=[mask_bf, token_bf, token_bf, token_bf],
            compiler_params=params(False),
            cost_estimate=estimate(),
            name="local_attention",
        )(*scalars, *near(queries, grad_normed, key_major, value_major), after, *near(*state))
        for kept, one in zip((query, grad, attended, entry, turned), made):
            kept.append(one)
        state[:] = [next_state]
        return tick

    entering, _ = pair_scan(
        list(states), False, scalars, rows, hops,
        [functools.partial(local_work, c) for c in range(steps)], 1,
    )

    *attended, sums = pl.pallas_call(
        functools.partial(sums_kernel, steps),
        in_specs=[SMEM, SMEM] + [VMEM] * (3 * steps + 5),
        out_specs=[VMEM] * (steps + 1),
        out_shape=[chunk_shape] * steps + [sums_shape],
        scratch_shapes=[held_bf, token_bf],
        input_output_aliases={3 + steps + c: c for c in range(steps)},
        compiler_params=params(False),
        cost_estimate=estimate(),
        name="token_sums",
    )(*scalars, norm_gain, *near(*query, *attended, *grad), *entering)
    sums = from_all(sums, "head")

    parts = 2 if hops == 1 else 4
    exit_shapes = [
        jax.ShapeDtypeStruct((heads // parts + (i == parts // 2), width, width), F32) for i in range(parts)
    ]
    *exits, gain_part = pl.pallas_call(
        functools.partial(exit_kernel, features, steps, len(sums), parts),
        in_specs=[SMEM, SMEM] + [VMEM] * (3 * steps + 1 + len(sums)),
        out_specs=[VMEM] * (parts + 1),
        out_shape=exit_shapes + [gain_shape],
        scratch_shapes=[token_f, token_f, held_f],
        compiler_params=params(False),
        cost_estimate=estimate(),
        name="start_grads",
    )(*scalars, norm_gain, *sums, *near(*turned, *attended, *grad))

    natives, key_local, value_local = [], [None] * steps, [None] * steps
    exit_state = []

    def grad_work(c, after):
        block = pl.BlockSpec((CHUNK, heads, width), lambda i: (c, 0, 0))
        given = [
            *scalars, *near(query[c], key_major, value_major, attended[c], grad[c], entry[c]),
            norm_gain, *entering, *sums, after, *near(*exit_state),
        ]
        *natives[:], key_local[c], value_local[c], next_state, tick = pl.pallas_call(
            functools.partial(grad_kernel, features, c, steps, len(sums)),
            grid=(1,),
            in_specs=[SMEM, SMEM] + [VMEM] * (11 + len(sums)) + [ANY] + [VMEM] * len(exit_state) + [HBM] * len(natives),
            out_specs=[block, block, VMEM, VMEM, VMEM, VMEM],
            out_shape=[native_shape, native_shape, chunk_shape, chunk_shape, held_f, tick_shape],
            scratch_shapes=[
                held_f, token_f, token_f, token_bf, token_bf, pltpu.VMEM((2, CHUNK, CHUNK), BF16),
                chunk_shape, chunk_shape,
            ],
            input_output_aliases={len(given) + i: i for i in range(len(natives))},
            compiler_params=params(),
            cost_estimate=estimate(),
            name="chunk_grads",
        )(*given, *natives)
        exit_state[:] = [next_state]
        return tick

    leaving, arrived = pair_scan(
        list(exits), True, scalars, rows, hops,
        [functools.partial(grad_work, c) for c in reversed(range(steps))], 1 if hops == 1 else 0,
    )
    normed, grad_queries = natives
    gains = [pair_gain(gain_part, arrived)]
    for distance in range(2, shards, 2):
        gains.append(lax.ppermute(gains[0], "ctx", [(i, i ^ distance) for i in range(shards)]))
    grad_gain = sum_gains(gains, key_local[0]) / math.sqrt(rows * shards)

    grad_keys, grad_values = pl.pallas_call(
        functools.partial(last_kernel, steps, parts),
        in_specs=[SMEM, SMEM] + [VMEM] * (2 * steps + 2 + parts),
        out_specs=[HBM] * 2,
        out_shape=[native_shape] * 2,
        scratch_shapes=[
            held_bf, token_bf, chunk_shape, chunk_shape,
            pltpu.VMEM((steps, CHUNK, heads, width), BF16),
            pltpu.VMEM((steps, CHUNK, heads, width), BF16),
            pltpu.SemaphoreType.DMA((2, steps)),
        ],
        compiler_params=params(False),
        cost_estimate=estimate(),
        name="key_grads",
    )(*scalars, *near(key_major, value_major, *key_local, *value_local), *leaving)
    return normed, grad_queries, grad_keys, grad_values, grad_gain


def solution(mesh):
    tokens = P("ctx", "head", None)
    in_specs = (tokens, tokens, tokens, tokens, P("head", None), P())
    out_specs = (tokens, tokens, tokens, tokens, P("head", None))
    return jax.shard_map(local, mesh=mesh, in_specs=in_specs, out_specs=out_specs, check_vma=False)
```
